32 devices in a mesh: ens: 2 (over y), tile: 4 (over z), chan: 2 (over x), sec: 2 (over core).
Axes of the slice: x: 2, y: 2, z: 4, core: 2. Of those that a mesh axis runs over, the one named last changes fastest.
Arguments:
- ocean_state: bfloat16 [256, 128, 4, 128], P(('chan', 'sec'), ('ens', 'tile')), parts along dimension 1, may hold values from -6 to 6
- atmos: bfloat16 [16384, 384], P(('ens', 'tile')), parts along dimension 0, may hold values from -6 to 6
- flux_weight: bfloat16 [384, 256], P(None, ('chan', 'sec')), may hold values from -0.3125 to 0.3125
- conv_weight: bfloat16 [9, 256, 256], P(None, None, ('chan', 'sec')), may hold values from -0.125 to 0.125
- conv_bias: bfloat16 [256], P(('chan', 'sec')), may hold values from -3 to 3
- norm_gain: bfloat16 [256], P(('chan', 'sec')), may hold values from 0.5 to 2
- in_weight: bfloat16 [256, 1024], P(None, ('chan', 'sec')), may hold values from -0.375 to 0.375
- in_bias: bfloat16 [1024], P(('chan', 'sec')), may hold values from -3 to 3
- out_weight: bfloat16 [1024, 256], P(('chan', 'sec')), may hold values from -0.25 to 0.25
- layer_scale: bfloat16 [256], P(('chan', 'sec')), may hold values from 0.5 to 2
- cell_mask: int32 [64, 4, 128], P('tile'), may hold values from 0 to 1, as said below
- neighbours: int32 [64, 8], P('tile'), may hold values from -1 to 63, as said below
- remap: int32 [64, 4, 128], P('tile'), may hold values from 0 to 8191
Outputs:
- ocean_next: bfloat16 [256, 128, 4, 128], P(('chan', 'sec'), ('ens', 'tile')), parts along dimension 1
The draws below stay inside these ranges and needn't reach their ends.
There are 2 independent parts, one for each index of `ens`. The reference program is written for one: setup_inputs(seed, part) draws one part's arguments, and reference() takes and returns one part's arrays. A program takes and returns all parts, laid end to end along the dimension named above; an argument that names none is the same for every part. Nothing has to cross between parts.
Inputs may be any that keep to these rules, and one draw needn't show every extreme that they name: `cell_mask`: land cells and every cell of a land block are 0. `neighbours`: for a slot among those of tile index t, each entry is -1 or a slot among those of tile indices t - 1, t and t + 1, i.e. in [(t - 1) * 16, (t + 2) * 16); entries that name land blocks are -1.
All inputs are finite; a program needn't handle non-finite values.
Results may differ from the reference program's by a relative error of at most 0.01.
Values may be sent and summed in bfloat16 or wider, within the bound.
A program may use at most 64 MiB of HBM per device.

```python
import math
import jax
import jax.numpy as jnp
from jax import lax

C = 256
HID = 1024
FA = 384
NB = 16
BH = 4
BW = 128
SLOTS = 64
ATM_ROWS = 8192
N_CHAN = 2
N_SEC = 2


def geography(key):
    device_count = SLOTS // NB
    key_order, key_land = jax.random.split(jax.random.fold_in(key, 7))
    scores = jax.random.randint(key_order, (device_count, NB), 0, 1 << 20) * NB + jnp.arange(NB, dtype=jnp.int32)[None, :]
    order = jnp.argsort(scores, axis=1).astype(jnp.int32)
    slot_of = jnp.argsort(order, axis=1).astype(jnp.int32)
    land = jax.random.randint(key_land, (device_count, NB), 0, 4) == 0
    return (order, slot_of, land)


def draw_neighbours(key, part):
    order, slot_of, land = geography(key)
    device_count = SLOTS // NB
    device_ids = jnp.zeros((device_count, NB), jnp.int32) + jnp.arange(device_count, dtype=jnp.int32)[:, None]
    block_row = device_ids
    block_col = order
    moves = [(0, -1), (0, 1), (-1, 0), (1, 0), (-1, -1), (-1, 1), (1, -1), (1, 1)]
    listed = []
    for move_row, move_col in moves:
        row_to = block_row + move_row
        col_to = block_col + move_col
        inside = (row_to >= 0) & (row_to < device_count) & (col_to >= 0) & (col_to < NB)
        col_safe = jnp.clip(col_to, 0, NB - 1)
        row_safe = jnp.clip(row_to, 0, device_count - 1)
        owner = row_safe
        local_block = col_safe
        target = owner * NB + slot_of[owner, local_block]
        live = inside & jnp.logical_not(land[owner, local_block])
        listed.append(jnp.where(live, target, -1))
    return jnp.stack(listed, axis=-1).reshape(SLOTS, 8).astype(jnp.int32)


def draw_cell_mask(key, part):
    order, slot_of, land = geography(key)
    land_slot = jnp.take_along_axis(land, order, axis=1).reshape(SLOTS)
    wet = jax.random.randint(jax.random.fold_in(key, 11), (SLOTS, BH, BW), 0, 8) != 0
    return (wet & jnp.logical_not(land_slot)[:, None, None]).astype(jnp.int32)


def set_ends(array, rng, smallest, top_value):
    longest = array.shape.index(max(array.shape))
    spots = []
    for shift in (0, 1):
        where = [jax.random.randint(jax.random.fold_in(rng, axis), (), 0, length) for axis, length in enumerate(array.shape)]
        where[longest] = (where[longest] + shift) % array.shape[longest]
        spots.append(tuple(where))
    return array.at[spots[0]].set(smallest).at[spots[1]].set(top_value)


def with_spikes(result, key, source, target, parts, factor):
    def block_of(dim):
        return (jnp.arange(result.shape[dim]) // (result.shape[dim] // parts)).reshape((-1,) + (1,) * (result.ndim - 1 - dim))

    first = jax.random.permutation(key, parts)[block_of(target)]
    far = (block_of(target) + parts // 2) % parts
    return jnp.where((block_of(source) == first) | (block_of(source) == far), factor * result, result)


def shard_levels(stream_key, shape, pieces, smallest, top_value):
    def one(position, blocks):
        draws = jax.random.uniform(jax.random.fold_in(jax.random.fold_in(stream_key, 6), position), (blocks,), jnp.float32, smallest / len(pieces), top_value / len(pieces))
        return jnp.repeat(jnp.exp(draws), shape[position] // blocks).reshape((-1,) + (1,) * (len(shape) - position - 1))

    loudness = one(*pieces[0])
    for cut in pieces[1:]:
        loudness = loudness * one(*cut)
    return loudness


def noise(rng, extent, deviation, bound, shards=(), held_as=jnp.bfloat16):
    entries = deviation * jax.random.normal(rng, extent, jnp.float32)
    if shards:
        entries = entries * shard_levels(rng, extent, shards, -0.22, 0.18)
    return jnp.clip(entries, -bound, bound).astype(held_as)


def gaussian_with(key, shape, deviation, most, pieces, heavy, held_as=jnp.bfloat16):
    drawn = deviation * jax.random.normal(key, shape, jnp.float32)
    if pieces:
        drawn = drawn * shard_levels(key, shape, pieces, -0.22, 0.18)
    return jnp.clip(with_spikes(drawn, jax.random.fold_in(key, 3), *heavy), -most, most).astype(held_as)


def setup_inputs(seed: int = 0, part: int = 0) -> dict:
    key_list = jax.random.split(jax.random.key(seed), 14)
    part_keys = jax.random.split(jax.random.fold_in(key_list[13], part), 14)
    return {
        "ocean_state": noise(part_keys[0], (C, SLOTS, BH, BW), 1.0, 6.0, ((0, 4), (1, 4))),
        "atmos": noise(part_keys[1], (ATM_ROWS, FA), 1.0, 6.0, ((0, 4),)),
        "flux_weight": noise(key_list[2], (FA, C), FA ** -0.5, 0.3125, ((1, 4),)),
        "conv_weight": noise(key_list[3], (9, C, C), (9 * C) ** -0.5, 0.125, ((2, 4),)),
        "conv_bias": noise(key_list[4], (C,), 0.5, 3.0, ((0, 4),)),
        "norm_gain": jnp.clip(jnp.exp(math.log(2.0) - 1.3862944 * jax.random.uniform(key_list[5], (C,), jnp.float32) ** shard_levels(key_list[5], (C,), ((0, 4),), -0.2, 0.2)), 0.5, 2.0).astype(jnp.bfloat16),
        "in_weight": noise(key_list[6], (C, HID), C ** -0.5, 0.375, ((1, 4),)),
        "in_bias": noise(key_list[7], (HID,), 0.5, 3.0, ((0, 4),)),
        "out_weight": gaussian_with(key_list[8], (HID, C), HID ** -0.5, 0.25, ((0, 4),), (0, 1, 4, 2.0)),
        "layer_scale": jnp.clip(jnp.exp(math.log(2.0) - 1.3862944 * jax.random.uniform(key_list[9], (C,), jnp.float32) ** shard_levels(key_list[9], (C,), ((0, 4),), -0.2, 0.2)), 0.5, 2.0).astype(jnp.bfloat16),
        "cell_mask": draw_cell_mask(jax.random.fold_in(key_list[13], 71), part),
        "neighbours": draw_neighbours(jax.random.fold_in(key_list[13], 71), part),
        "remap": set_ends(jax.random.randint(key_list[12], (SLOTS, BH, BW), 0, ATM_ROWS), jax.random.fold_in(key_list[12], 1), 0, ATM_ROWS - 1).astype(jnp.int32),
    }


norm_eps = 1e-06

def strips_of(state):
    return jnp.concatenate([state[:, :, 0, :], state[:, :, -1, :], state[:, :, :, 0], state[:, :, :, -1], state[:, :, 0, 0:1], state[:, :, 0, -1:], state[:, :, -1, 0:1], state[:, :, -1, -1:]], axis=2)

def pad_blocks(state, strips, slot_index, valid):
    channels, slot_count, block_rows, block_cols = state.shape
    width = strips.shape[2]
    picked = jnp.take(strips, slot_index.reshape(-1), axis=1).reshape(channels, slot_count, 8, width)
    picked = jnp.where(valid[None, :, :, None], picked, jnp.zeros_like(picked))
    offset_base = 2 * block_cols + 2 * block_rows
    west_col = picked[:, :, 0, 2 * block_cols + block_rows:offset_base]
    east_col = picked[:, :, 1, 2 * block_cols:2 * block_cols + block_rows]
    prev_row = picked[:, :, 2, block_cols:2 * block_cols]
    next_row = picked[:, :, 3, 0:block_cols]
    top_row = jnp.concatenate([picked[:, :, 4, offset_base + 3:offset_base + 4], prev_row, picked[:, :, 5, offset_base + 2:offset_base + 3]], axis=2)
    bottom_row = jnp.concatenate([picked[:, :, 6, offset_base + 1:offset_base + 2], next_row, picked[:, :, 7, offset_base:offset_base + 1]], axis=2)
    middle = jnp.concatenate([west_col[:, :, :, None], state, east_col[:, :, :, None]], axis=3)
    return jnp.concatenate([top_row[:, :, None, :], middle, bottom_row[:, :, None, :]], axis=2)

def conv_taps(padded, kernel, block_rows, block_cols):
    padded = padded.astype(jnp.float32)
    kernel = kernel.astype(jnp.float32)
    total = jnp.zeros((kernel.shape[2], padded.shape[1], block_rows, block_cols), jnp.float32)
    for tap in range(9):
        tap_row = tap // 3
        tap_col = tap % 3
        window = padded[:, :, tap_row:tap_row + block_rows, tap_col:tap_col + block_cols]
        total = total + jnp.einsum('cskl,co->oskl', window, kernel[tap])
    return total

def reference(ocean_state, atmos, flux_weight, conv_weight, conv_bias, norm_gain, in_weight, in_bias, out_weight, layer_scale, cell_mask, neighbours, remap):
    valid = neighbours >= 0
    slot_index = jnp.clip(neighbours, 0, SLOTS - 1).astype(jnp.int32)
    padded = pad_blocks(ocean_state, strips_of(ocean_state), slot_index, valid)
    conv_out = conv_taps(padded, conv_weight, BH, BW) + conv_bias.astype(jnp.float32)[:, None, None, None]
    squares = lax.optimization_barrier(jnp.sum(conv_out * conv_out, axis=0))
    normed = (conv_out * lax.rsqrt(squares / C + norm_eps) * norm_gain.astype(jnp.float32)[:, None, None, None]).astype(jnp.bfloat16)
    pre = jnp.einsum('csij,ch->hsij', normed.astype(jnp.float32), in_weight.astype(jnp.float32))
    hidden = jax.nn.gelu(pre + in_bias.astype(jnp.float32)[:, None, None, None], approximate=False).astype(jnp.bfloat16)
    groups = N_CHAN * N_SEC
    hid_groups = hidden.reshape(groups, HID // groups, SLOTS, BH, BW)
    out_groups = out_weight.reshape(groups, HID // groups, C)

    def add_group(total, pair):
        term = jnp.einsum('hsij,hc->csij', pair[0].astype(jnp.float32), pair[1].astype(jnp.float32)).astype(jnp.bfloat16)
        term = lax.optimization_barrier(term)
        return (total + term.astype(jnp.float32), None)
    update, _ = lax.scan(add_group, jnp.zeros((C, SLOTS, BH, BW), jnp.float32), (hid_groups, out_groups))
    fluxes = jnp.dot(atmos, flux_weight, preferred_element_type=jnp.float32).astype(jnp.bfloat16)
    forcing = jnp.take(fluxes, remap.reshape(-1).astype(jnp.int32), axis=0).T.reshape(C, SLOTS, BH, BW)
    total = ocean_state.astype(jnp.float32) + layer_scale.astype(jnp.float32)[:, None, None, None] * update + forcing.astype(jnp.float32)
    return (cell_mask.astype(jnp.float32)[None] * total).astype(jnp.bfloat16)
```

```python
import functools

import jax
import jax.numpy as jnp
from jax import lax
from jax.experimental import pallas as pl
from jax.experimental.pallas import tpu as pltpu
from jax.sharding import PartitionSpec as P

norm_eps = 1e-06
F32, BF16 = jnp.float32, jnp.bfloat16
LIMIT = 48 * 1024 * 1024


def params():
    return pltpu.CompilerParams(vmem_limit_bytes=LIMIT)


def nt(a, b):
    return lax.dot_general(a, b, (((1,), (1,)), ((), ())), preferred_element_type=F32)


def whole(*shape):
    return pl.BlockSpec(shape, lambda *_: (0,) * len(shape))


def eye(n, m, off=0):
    r = lax.broadcasted_iota(jnp.int32, (n, m), 0)
    c = lax.broadcasted_iota(jnp.int32, (n, m), 1)
    return jnp.where(c == r + off, 1.0, 0.0).astype(BF16)


def pack_weights(cw, vec, iw, ow, out):
    taps, chan, cl = cw.shape
    hl = iw.shape[1]
    for t in range(taps):
        out[t * cl : (t + 1) * cl, :] = cw[t].astype(F32).T.astype(BF16)
    base = taps * cl
    out[base : base + hl, :] = iw[...].astype(F32).T.astype(BF16)
    out[base + hl : base + 2 * hl, :] = ow[...]
    out[base + 2 * hl :, :] = vec[...]


def flux_rows(atm, fw, out):
    cl = fw.shape[1]
    rows = out.shape[0]
    w = fw[...]
    parts = []
    for k in range(atm.shape[0] // rows):
        parts.append(jnp.dot(atm[k * rows : (k + 1) * rows, :], w, preferred_element_type=F32))
    out[...] = jnp.concatenate(parts, axis=1).astype(BF16)


def split_rows(state, rows_out, strips, scr):
    s = pl.program_id(0)
    slots = pl.num_programs(0)
    cl, _, bh, bw = state.shape
    scr[...] = state[:, 0].astype(F32)

    @pl.when(s == 0)
    def _():
        strips[slots] = jnp.zeros(strips.shape[1:], BF16)

    lane = lax.broadcasted_iota(jnp.int32, (cl, bw), 1)
    edge = strips[slots, :, 0:bw].astype(F32)
    for i in range(bh):
        row = scr[:, i, :]
        edge = jnp.where(lane == s * 8 + i, row[:, 0:1], edge)
        edge = jnp.where(lane == s * 8 + 4 + i, row[:, bw - 1 : bw], edge)
        cells = row.astype(BF16)
        rows_out[0, :, i * bw : (i + 1) * bw] = cells
        if i == 0:
            strips[s, :, 0:bw] = cells
        if i == bh - 1:
            strips[s, :, bw : 2 * bw] = cells
    strips[slots, :, 0:bw] = edge.astype(BF16)


def halo(near, rows, below, mine, above, out, ext):
    s = pl.program_id(0)
    slots = pl.num_programs(0)
    cl = rows.shape[1]
    bw = 128
    width = rows.shape[2]

    @pl.when(s == 0)
    def _():
        ext[0] = below[...]
        ext[1] = mine[...]
        ext[2] = above[...]

    lane = lax.broadcasted_iota(jnp.int32, (cl, bw), 1)

    def place(k):
        n = near[s, k]
        ok = n >= 0
        m = jnp.maximum(n, 0)
        return ok, m // slots, lax.rem(m, slots)

    def strip(k, lo):
        ok, t, m = place(k)
        got = ext[t, m, :, lo : lo + bw].astype(F32)
        return jnp.where(ok, got, 0.0).astype(BF16)

    out[0, :, 0:bw] = strip(2, bw)
    out[0, :, bw : bw + width] = rows[0]
    out[0, :, bw + width : 2 * bw + width] = strip(3, 0)
    edge = jnp.zeros((cl, bw), F32)
    for k, src, dst, count in (
        (4, 7, 0, 1), (0, 4, 1, 4), (6, 4, 5, 1), (5, 3, 6, 1), (1, 0, 7, 4), (7, 0, 11, 1),
    ):
        ok, t, m = place(k)
        turned = pltpu.roll(
            ext[t, slots, :, 0:bw].astype(F32), lax.rem(dst - src - m * 8 + 2 * bw, bw), 1
        )
        here = (lane >= dst) & (lane < dst + count)
        edge = jnp.where(here, jnp.where(ok, turned, 0.0), edge)
    out[0, :, 2 * bw + width :] = edge.astype(BF16)


def block(tile, pack, out, xs, hid, *, hl):
    groups, _, cl, width = tile.shape
    chan = groups * cl
    bw = 128
    rows = width // bw - 1
    cells = (rows - 2) * bw
    x = tile[:, 0].reshape(chan, width)
    edge = x[:, rows * bw :].astype(F32)
    lane = lax.broadcasted_iota(jnp.int32, (chan, bw), 1)
    for i in range(rows):
        mid = x[:, i * bw : (i + 1) * bw]
        wide = mid.astype(F32)
        left = jnp.where(lane == 0, edge[:, i : i + 1], pltpu.roll(wide, 1, 1))
        right = jnp.where(lane == bw - 1, edge[:, rows + i : rows + i + 1], pltpu.roll(wide, bw - 1, 1))
        at = slice(i * bw, (i + 1) * bw)
        xs[0:chan, at] = left.astype(BF16)
        xs[chan : 2 * chan, at] = mid
        xs[2 * chan : 3 * chan, at] = right.astype(BF16)
    base = 9 * cl
    ident = eye(256, 256)
    cols = [nt(ident, pack[g, base + 2 * hl :, :]) for g in range(groups)]
    bias = jnp.concatenate([c[:cl, 1:2] for c in cols], axis=0)
    gain = jnp.concatenate([c[:cl, 2:3] for c in cols], axis=0)
    acc = jnp.zeros((chan, cells), F32)
    for a in range(3):
        for b in range(3):
            t = 3 * a + b
            w = pack[:, t * cl : (t + 1) * cl, :].reshape(chan, chan)
            acc += jnp.dot(
                w, xs[b * chan : (b + 1) * chan, a * bw : a * bw + cells], preferred_element_type=F32
            )
    acc = acc + bias
    squares = jnp.sum(acc * acc, axis=0, keepdims=True)
    normed = (acc * lax.rsqrt(squares / chan + norm_eps) * gain).astype(BF16)
    for g in range(groups):
        pre = jnp.dot(pack[g, base : base + hl, :], normed, preferred_element_type=F32)
        pre = pre + cols[g][:hl, 0:1]
        act = 0.5 * pre * (1.0 + lax.erf(pre * 0.7071067811865476))
        hid[g * hl : (g + 1) * hl, :] = act.astype(BF16)
    ow = pack[:, base + hl : base + 2 * hl, :].reshape(groups * hl, chan)
    upd = lax.dot_general(ow, hid[...], (((0,), (0,)), ((), ())), preferred_element_type=F32)
    out[:, 0] = upd.astype(BF16).reshape(groups, cl, cells)


def pick(index, table, which, out, wide, got, *, cl):
    s = pl.program_id(0)
    cells = got.shape[0]
    parts = 128 // cl

    @pl.when(s == 0)
    def _():
        wide[...] = table[...].astype(F32)

    def body(j, c):
        for u in range(16):
            at = j * 16 + u
            got[pl.ds(at, 1), :] = wide[pl.ds(index[s * cells + at], 1), :]
        return c

    lax.fori_loop(0, cells // 16, body, 0)
    rows = got[...].astype(BF16)
    part = which[0]
    total = jnp.zeros((cl, cells), F32)
    for k in range(parts):
        total = jnp.where(part == k, nt(eye(cl, 128, k * cl), rows), total)
    out[0] = total.astype(BF16)


def finish(rows, update, force, mask, scale, out, scr):
    cl, _, bh, bw = out.shape
    total = rows[0].astype(F32) + scale[:, 0:1].astype(F32) * update[0].astype(F32)
    total = (total + force[0].astype(F32)) * mask[0].astype(F32)
    for i in range(bh):
        scr[:, i, :] = total[:, i * bw : (i + 1) * bw]
    out[:, 0] = scr[...].astype(BF16)


def on_device(
    ocean_state, atmos, flux_weight, conv_weight, conv_bias, norm_gain, in_weight, in_bias,
    out_weight, layer_scale, cell_mask, neighbours, remap,
):
    cl, slots, bh, bw = ocean_state.shape
    groups = lax.axis_size(("chan", "sec"))
    tiles = lax.axis_size("tile")
    chan = groups * cl
    hl = in_weight.shape[1]
    cells = bh * bw
    per = slots // groups
    width = cells + 3 * bw

    state_spec = pl.BlockSpec((cl, 1, bh, bw), lambda s, *_: (0, s, 0, 0))
    slot_spec = pl.BlockSpec((1, cl, cells), lambda s, *_: (s, 0, 0))
    rows, strips = pl.pallas_call(
        split_rows,
        grid=(slots,),
        in_specs=[state_spec],
        out_specs=[slot_spec, whole(slots + 1, cl, 2 * bw)],
        out_shape=[
            jax.ShapeDtypeStruct((slots, cl, cells), BF16),
            jax.ShapeDtypeStruct((slots + 1, cl, 2 * bw), BF16),
        ],
        scratch_shapes=[pltpu.VMEM((cl, bh, bw), F32)],
        compiler_params=params(),
        name="split_rows",
    )(ocean_state)
    below = lax.ppermute(strips, "tile", [(i, i + 1) for i in range(tiles - 1)])
    above = lax.ppermute(strips, "tile", [(i + 1, i) for i in range(tiles - 1)])

    vec = jnp.stack(
        [jnp.pad(v, (0, chan - v.shape[0])) for v in (in_bias, conv_bias, norm_gain)]
    )
    vec = jnp.pad(vec, ((0, 13), (0, 0)))
    pack_rows = 9 * cl + 2 * hl + 16
    pack = pl.pallas_call(
        pack_weights,
        out_shape=jax.ShapeDtypeStruct((pack_rows, chan), BF16),
        compiler_params=params(),
        name="pack_weights",
    )(conv_weight, vec, in_weight, out_weight)
    pack = lax.all_gather(pack, ("chan", "sec"), axis=0)

    parts = 128 // cl
    trows = atmos.shape[0] // parts
    table = pl.pallas_call(
        flux_rows,
        out_shape=jax.ShapeDtypeStruct((trows, 128), BF16),
        compiler_params=params(),
        name="flux_rows",
    )(atmos, flux_weight)
    table = lax.all_gather(table, "tile", axis=0, tiled=True)

    local = lax.rem(remap, trows * parts)
    flat = (remap // (trows * parts)) * trows + lax.rem(local, trows)
    which = (local // trows).reshape(slots, 1, cells)
    lane_spec = pl.BlockSpec((1, 1, cells), lambda s, *_: (s, 0, 0))
    forcing = pl.pallas_call(
        functools.partial(pick, cl=cl),
        grid_spec=pltpu.PrefetchScalarGridSpec(
            num_scalar_prefetch=1,
            grid=(slots,),
            in_specs=[whole(tiles * trows, 128), lane_spec],
            out_specs=slot_spec,
            scratch_shapes=[pltpu.VMEM((tiles * trows, 128), F32), pltpu.VMEM((cells, 128), F32)],
        ),
        out_shape=jax.ShapeDtypeStruct((slots, cl, cells), BF16),
        compiler_params=params(),
        cost_estimate=pl.CostEstimate(flops=10**10, bytes_accessed=4 * 10**6, transcendentals=0),
        name="pick",
    )(flat.reshape(-1), table, which)

    first = (lax.axis_index("tile") - 1) * slots
    near = jnp.where(neighbours >= 0, jnp.clip(neighbours - first, 0, 3 * slots - 1), -1)
    strip_spec = whole(slots + 1, cl, 2 * bw)
    padded = pl.pallas_call(
        halo,
        grid_spec=pltpu.PrefetchScalarGridSpec(
            num_scalar_prefetch=1,
            grid=(slots,),
            in_specs=[slot_spec, strip_spec, strip_spec, strip_spec],
            out_specs=pl.BlockSpec((1, cl, width), lambda s, *_: (s, 0, 0)),
            scratch_shapes=[pltpu.VMEM((3, slots + 1, cl, 2 * bw), BF16)],
        ),
        out_shape=jax.ShapeDtypeStruct((slots, cl, width), BF16),
        compiler_params=params(),
        name="halo",
    )(near, rows, below, strips, above)
    tile = lax.all_to_all(
        padded.reshape(groups, per, cl, width), ("chan", "sec"), split_axis=0, concat_axis=0
    )
    update = pl.pallas_call(
        functools.partial(block, hl=hl),
        grid=(per,),
        in_specs=[
            pl.BlockSpec((groups, 1, cl, width), lambda s: (0, s, 0, 0)),
            whole(groups, pack_rows, chan),
        ],
        out_specs=pl.BlockSpec((groups, 1, cl, cells), lambda s: (0, s, 0, 0)),
        out_shape=jax.ShapeDtypeStruct((groups, per, cl, cells), BF16),
        scratch_shapes=[
            pltpu.VMEM((3 * chan, (bh + 2) * bw), BF16),
            pltpu.VMEM((groups * hl, cells), BF16),
        ],
        compiler_params=params(),
        name="block",
    )(tile, pack)
    update = lax.all_to_all(update, ("chan", "sec"), split_axis=0, concat_axis=0)
    return pl.pallas_call(
        finish,
        grid=(slots,),
        in_specs=[slot_spec, slot_spec, slot_spec, lane_spec, whole(cl, 1)],
        out_specs=state_spec,
        out_shape=jax.ShapeDtypeStruct(ocean_state.shape, BF16),
        scratch_shapes=[pltpu.VMEM((cl, bh, bw), F32)],
        compiler_params=params(),
        name="finish",
    )(
        rows,
        update.reshape(slots, cl, cells),
        forcing,
        cell_mask.reshape(slots, 1, cells),
        layer_scale.reshape(cl, 1),
    )


def solution(mesh):
    placed = (
        P(("chan", "sec"), ("ens", "tile"), None, None),
        P(("ens", "tile"), None),
        P(None, ("chan", "sec")),
        P(None, None, ("chan", "sec")),
        P(("chan", "sec")),
        P(("chan", "sec")),
        P(None, ("chan", "sec")),
        P(("chan", "sec")),
        P(("chan", "sec"), None),
        P(("chan", "sec")),
        P("tile", None, None),
        P("tile", None),
        P("tile", None, None),
    )
    return jax.shard_map(
        on_device,
        mesh=mesh,
        in_specs=placed,
        out_specs=P(("chan", "sec"), ("ens", "tile"), None, None),
        check_vma=False,
    )
```

```python
import functools

import jax
import jax.numpy as jnp
from jax import lax
from jax.experimental import pallas as pl
from jax.experimental.pallas import tpu as pltpu
from jax.sharding import PartitionSpec as P

norm_eps = 1e-06
F32, BF16 = jnp.float32, jnp.bfloat16
LIMIT = 48 * 1024 * 1024


def params():
    return pltpu.CompilerParams(vmem_limit_bytes=LIMIT)


def nt(a, b):
    return lax.dot_general(a, b, (((1,), (1,)), ((), ())), preferred_element_type=F32)


def whole(*shape):
    return pl.BlockSpec(shape, lambda *_: (0,) * len(shape))


def eye(n, m, off=0):
    r = lax.broadcasted_iota(jnp.int32, (n, m), 0)
    c = lax.broadcasted_iota(jnp.int32, (n, m), 1)
    return jnp.where(c == r + off, 1.0, 0.0).astype(BF16)


def pack_weights(cw, vec, iw, ow, out):
    taps, chan, cl = cw.shape
    hl = iw.shape[1]
    for t in range(taps):
        out[t * cl : (t + 1) * cl, :] = cw[t].astype(F32).T.astype(BF16)
    base = taps * cl
    out[base : base + hl, :] = iw[...].astype(F32).T.astype(BF16)
    out[base + hl : base + 2 * hl, :] = ow[...]
    out[base + 2 * hl :, :] = vec[...]


def flux_rows(atm, fw, out):
    cl = fw.shape[1]
    rows = out.shape[0]
    w = fw[...]
    parts = []
    for k in range(atm.shape[0] // rows):
        parts.append(jnp.dot(atm[k * rows : (k + 1) * rows, :], w, preferred_element_type=F32))
    out[...] = jnp.concatenate(parts, axis=1).astype(BF16)


def split_rows(state, rows_out, strips, scr):
    s = pl.program_id(0)
    cl, some, bh, bw = state.shape
    last = strips.shape[0] - 1

    @pl.when(s == 0)
    def _():
        strips[last] = jnp.zeros(strips.shape[1:], BF16)

    lane = lax.broadcasted_iota(jnp.int32, (cl, bw), 1)
    edge = strips[last, :, 0:bw].astype(F32)
    for j in range(some):
        scr[...] = state[:, j].astype(F32)
        slot = s * some + j
        for i in range(bh):
            row = scr[:, i, :]
            edge = jnp.where(lane == slot * 8 + i, row[:, 0:1], edge)
            edge = jnp.where(lane == slot * 8 + 4 + i, row[:, bw - 1 : bw], edge)
            cells = row.astype(BF16)
            rows_out[j, :, i * bw : (i + 1) * bw] = cells
            if i == 0:
                strips[slot, :, 0:bw] = cells
            if i == bh - 1:
                strips[slot, :, bw : 2 * bw] = cells
    strips[last, :, 0:bw] = edge.astype(BF16)


def halo(near, below, mine, above, out, *, per):
    g = pl.program_id(0)
    slots = per * pl.num_programs(0)
    cl = out.shape[2]
    bw = 128
    lane = lax.broadcasted_iota(jnp.int32, (cl, bw), 1)

    def choose(t, m, at):
        got = jnp.where(t == 1, mine[m, :, at].astype(F32), below[m, :, at].astype(F32))
        return jnp.where(t == 2, above[m, :, at].astype(F32), got)

    edge = jnp.zeros((cl, bw), F32)
    for j in range(per):

        def place(k):
            n = near[g * per + j, k]
            m = jnp.maximum(n, 0)
            return n >= 0, m // slots, lax.rem(m, slots)

        for k, lo, unit in ((2, bw, 0), (3, 0, 1)):
            ok, t, m = place(k)
            got = choose(t, m, slice(lo, lo + bw))
            out[0, 2 * j + unit] = jnp.where(ok, got, 0.0).astype(BF16)
        for k, src, dst, count in (
            (4, 7, 0, 1), (0, 4, 1, 4), (6, 4, 5, 1), (5, 3, 6, 1), (1, 0, 7, 4), (7, 0, 11, 1),
        ):
            ok, t, m = place(k)
            to = j * 12 + dst
            turned = pltpu.roll(
                choose(t, slots, slice(0, bw)), lax.rem(to - src - m * 8 + 2 * bw, bw), 1
            )
            here = (lane >= to) & (lane < to + count)
            edge = jnp.where(here, jnp.where(ok, turned, 0.0), edge)
    out[0, 2 * per] = edge.astype(BF16)


def block(tile, rim, pack, out, xs, hid, *, hl):
    groups, _, cl, cells = tile.shape
    chan = groups * cl
    bw = 128
    rows = cells // bw + 2
    s = pl.program_id(0)
    edge = rim[:, rim.shape[1] - 1].reshape(chan, bw).astype(F32)
    edge = pltpu.roll(edge, lax.rem(bw - s * 12, bw), 1)
    lane = lax.broadcasted_iota(jnp.int32, (chan, bw), 1)
    for i in range(rows):
        if i == 0:
            mid = rim[:, 2 * s].reshape(chan, bw)
        elif i == rows - 1:
            mid = rim[:, 2 * s + 1].reshape(chan, bw)
        else:
            mid = tile[:, 0, :, (i - 1) * bw : i * bw].reshape(chan, bw)
        wide = mid.astype(F32)
        left = jnp.where(lane == 0, edge[:, i : i + 1], pltpu.roll(wide, 1, 1))
        right = jnp.where(lane == bw - 1, edge[:, rows + i : rows + i + 1], pltpu.roll(wide, bw - 1, 1))
        at = slice(i * bw, (i + 1) * bw)
        xs[0:chan, at] = left.astype(BF16)
        xs[chan : 2 * chan, at] = mid
        xs[2 * chan : 3 * chan, at] = right.astype(BF16)
    base = 9 * cl
    ident = eye(256, 256)
    cols = [nt(ident, pack[g, base + 2 * hl :, :]) for g in range(groups)]
    bias = jnp.concatenate([c[:cl, 1:2] for c in cols], axis=0)
    gain = jnp.concatenate([c[:cl, 2:3] for c in cols], axis=0)
    acc = jnp.zeros((chan, cells), F32)
    for a in range(3):
        for b in range(3):
            t = 3 * a + b
            w = pack[:, t * cl : (t + 1) * cl, :].reshape(chan, chan)
            acc += jnp.dot(
                w, xs[b * chan : (b + 1) * chan, a * bw : a * bw + cells], preferred_element_type=F32
            )
    acc = acc + bias
    squares = jnp.sum(acc * acc, axis=0, keepdims=True)
    normed = (acc * lax.rsqrt(squares / chan + norm_eps) * gain).astype(BF16)
    for g in range(groups):
        pre = jnp.dot(pack[g, base : base + hl, :], normed, preferred_element_type=F32)
        pre = pre + cols[g][:hl, 0:1]
        act = 0.5 * pre * (1.0 + lax.erf(pre * 0.7071067811865476))
        hid[g * hl : (g + 1) * hl, :] = act.astype(BF16)
    ow = pack[:, base + hl : base + 2 * hl, :].reshape(groups * hl, chan)
    upd = lax.dot_general(ow, hid[...], (((0,), (0,)), ((), ())), preferred_element_type=F32)
    out[:, 0] = upd.astype(BF16).reshape(groups, cl, cells)


def pick(index, table, which, out, wide, got, *, cl):
    s = pl.program_id(0)
    cells = got.shape[0]
    parts = 128 // cl

    @pl.when(s == 0)
    def _():
        wide[...] = table[...].astype(F32)

    def body(j, c):
        for u in range(16):
            at = j * 16 + u
            got[pl.ds(at, 1), :] = wide[pl.ds(index[s * cells + at], 1), :]
        return c

    lax.fori_loop(0, cells // 16, body, 0)
    rows = got[...].astype(BF16)
    part = which[0]
    total = jnp.zeros((cl, cells), F32)
    for k in range(parts):
        total = jnp.where(part == k, nt(eye(cl, 128, k * cl), rows), total)
    out[0] = total.astype(BF16)


def finish(rows, update, force, mask, scale, out, scr):
    cl, some, bh, bw = out.shape
    gain = scale[:, 0:1].astype(F32)
    for j in range(some):
        total = rows[j].astype(F32) + gain * update[j].astype(F32)
        total = (total + force[j].astype(F32)) * mask[j].astype(F32)
        for i in range(bh):
            scr[:, i, :] = total[:, i * bw : (i + 1) * bw]
        out[:, j] = scr[...].astype(BF16)


def on_device(
    ocean_state, atmos, flux_weight, conv_weight, conv_bias, norm_gain, in_weight, in_bias,
    out_weight, layer_scale, cell_mask, neighbours, remap,
):
    cl, slots, bh, bw = ocean_state.shape
    groups = lax.axis_size(("chan", "sec"))
    tiles = lax.axis_size("tile")
    chan = groups * cl
    hl = in_weight.shape[1]
    cells = bh * bw
    per = slots // groups
    some = 4

    state_spec = pl.BlockSpec((cl, some, bh, bw), lambda s, *_: (0, s, 0, 0))
    some_spec = pl.BlockSpec((some, cl, cells), lambda s, *_: (s, 0, 0))
    slot_spec = pl.BlockSpec((1, cl, cells), lambda s, *_: (s, 0, 0))
    rows, strips = pl.pallas_call(
        split_rows,
        grid=(slots // some,),
        in_specs=[state_spec],
        out_specs=[some_spec, whole(slots + 1, cl, 2 * bw)],
        out_shape=[
            jax.ShapeDtypeStruct((slots, cl, cells), BF16),
            jax.ShapeDtypeStruct((slots + 1, cl, 2 * bw), BF16),
        ],
        scratch_shapes=[pltpu.VMEM((cl, bh, bw), F32)],
        compiler_params=params(),
        name="split_rows",
    )(ocean_state)
    tile = lax.all_to_all(
        rows.reshape(groups, per, cl, cells), ("chan", "sec"), split_axis=0, concat_axis=0
    )
    below = lax.ppermute(strips, "tile", [(i, i + 1) for i in range(tiles - 1)])
    above = lax.ppermute(strips, "tile", [(i + 1, i) for i in range(tiles - 1)])

    vec = jnp.stack(
        [jnp.pad(v, (0, chan - v.shape[0])) for v in (in_bias, conv_bias, norm_gain)]
    )
    vec = jnp.pad(vec, ((0, 13), (0, 0)))
    pack_rows = 9 * cl + 2 * hl + 16
    pack = pl.pallas_call(
        pack_weights,
        out_shape=jax.ShapeDtypeStruct((pack_rows, chan), BF16),
        compiler_params=params(),
        name="pack_weights",
    )(conv_weight, vec, in_weight, out_weight)
    pack = lax.all_gather(pack, ("chan", "sec"), axis=0)

    below, above, atmos = lax.optimization_barrier((below, above, atmos))
    parts = 128 // cl
    trows = atmos.shape[0] // parts
    table = pl.pallas_call(
        flux_rows,
        out_shape=jax.ShapeDtypeStruct((trows, 128), BF16),
        compiler_params=params(),
        name="flux_rows",
    )(atmos, flux_weight)
    table = lax.all_gather(table, "tile", axis=0, tiled=True)

    local = lax.rem(remap, trows * parts)
    flat = (remap // (trows * parts)) * trows + lax.rem(local, trows)
    which = (local // trows).reshape(slots, 1, cells)
    lane_spec = pl.BlockSpec((1, 1, cells), lambda s, *_: (s, 0, 0))
    forcing = pl.pallas_call(
        functools.partial(pick, cl=cl),
        grid_spec=pltpu.PrefetchScalarGridSpec(
            num_scalar_prefetch=1,
            grid=(slots,),
            in_specs=[whole(tiles * trows, 128), lane_spec],
            out_specs=slot_spec,
            scratch_shapes=[pltpu.VMEM((tiles * trows, 128), F32), pltpu.VMEM((cells, 128), F32)],
        ),
        out_shape=jax.ShapeDtypeStruct((slots, cl, cells), BF16),
        compiler_params=params(),
        cost_estimate=pl.CostEstimate(flops=10**10, bytes_accessed=4 * 10**6, transcendentals=0),
        name="pick",
    )(flat.reshape(-1), table, which)

    first = (lax.axis_index("tile") - 1) * slots
    near = jnp.where(neighbours >= 0, jnp.clip(neighbours - first, 0, 3 * slots - 1), -1)
    strip_spec = whole(slots + 1, cl, 2 * bw)
    units = 2 * per + 1
    rim = pl.pallas_call(
        functools.partial(halo, per=per),
        grid_spec=pltpu.PrefetchScalarGridSpec(
            num_scalar_prefetch=1,
            grid=(groups,),
            in_specs=[strip_spec, strip_spec, strip_spec],
            out_specs=pl.BlockSpec((1, units, cl, bw), lambda s, *_: (s, 0, 0, 0)),
        ),
        out_shape=jax.ShapeDtypeStruct((groups, units, cl, bw), BF16),
        compiler_params=params(),
        name="halo",
    )(near, below, strips, above)
    rim = lax.all_to_all(rim, ("chan", "sec"), split_axis=0, concat_axis=0)
    update = pl.pallas_call(
        functools.partial(block, hl=hl),
        grid=(per,),
        in_specs=[
            pl.BlockSpec((groups, 1, cl, cells), lambda s: (0, s, 0, 0)),
            whole(groups, units, cl, bw),
            whole(groups, pack_rows, chan),
        ],
        out_specs=pl.BlockSpec((groups, 1, cl, cells), lambda s: (0, s, 0, 0)),
        out_shape=jax.ShapeDtypeStruct((groups, per, cl, cells), BF16),
        scratch_shapes=[
            pltpu.VMEM((3 * chan, (bh + 2) * bw), BF16),
            pltpu.VMEM((groups * hl, cells), BF16),
        ],
        compiler_params=params(),
        name="block",
    )(tile, rim, pack)
    update = lax.all_to_all(update, ("chan", "sec"), split_axis=0, concat_axis=0)
    return pl.pallas_call(
        finish,
        grid=(slots // some,),
        in_specs=[
            some_spec, some_spec, some_spec,
            pl.BlockSpec((some, 1, cells), lambda s: (s, 0, 0)), whole(cl, 1),
        ],
        out_specs=state_spec,
        out_shape=jax.ShapeDtypeStruct(ocean_state.shape, BF16),
        scratch_shapes=[pltpu.VMEM((cl, bh, bw), F32)],
        compiler_params=params(),
        name="finish",
    )(
        rows,
        update.reshape(slots, cl, cells),
        forcing,
        cell_mask.reshape(slots, 1, cells),
        layer_scale.reshape(cl, 1),
    )


def solution(mesh):
    placed = (
        P(("chan", "sec"), ("ens", "tile"), None, None),
        P(("ens", "tile"), None),
        P(None, ("chan", "sec")),
        P(None, None, ("chan", "sec")),
        P(("chan", "sec")),
        P(("chan", "sec")),
        P(None, ("chan", "sec")),
        P(("chan", "sec")),
        P(("chan", "sec"), None),
        P(("chan", "sec")),
        P("tile", None, None),
        P("tile", None),
        P("tile", None, None),
    )
    return jax.shard_map(
        on_device,
        mesh=mesh,
        in_specs=placed,
        out_specs=P(("chan", "sec"), ("ens", "tile"), None, None),
        check_vma=False,
    )
```

```python
import functools

import jax
import jax.numpy as jnp
from jax import lax
from jax.experimental import pallas as pl
from jax.experimental.pallas import tpu as pltpu
from jax.sharding import PartitionSpec as P

norm_eps = 1e-06
F32, BF16 = jnp.float32, jnp.bfloat16
LIMIT = 48 * 1024 * 1024


def params():
    return pltpu.CompilerParams(vmem_limit_bytes=LIMIT)


def nt(a, b):
    return lax.dot_general(a, b, (((1,), (1,)), ((), ())), preferred_element_type=F32)


def whole(*shape):
    return pl.BlockSpec(shape, lambda *_: (0,) * len(shape))


def eye(n, m, off=0):
    r = lax.broadcasted_iota(jnp.int32, (n, m), 0)
    c = lax.broadcasted_iota(jnp.int32, (n, m), 1)
    return jnp.where(c == r + off, 1.0, 0.0).astype(BF16)


def pack_weights(cw, vec, iw, ow, out):
    taps, cl, chan = cw.shape
    hl = iw.shape[1]
    for t in range(taps):
        out[t * cl : (t + 1) * cl, :] = cw[t]
    base = taps * cl
    out[base : base + hl, :] = iw[...].astype(F32).T.astype(BF16)
    out[base + hl : base + 2 * hl, :] = ow[...]
    out[base + 2 * hl :, :] = vec[...]


def flux_rows(atm, fw, out):
    rows = out.shape[0]
    w = fw[...]
    parts = []
    for k in range(atm.shape[0] // rows):
        parts.append(nt(atm[k * rows : (k + 1) * rows, :], w))
    out[...] = jnp.concatenate(parts, axis=1).astype(BF16)


def split_rows(state, rows_out, strips, scr):
    s = pl.program_id(0)
    cl, some, bh, bw = state.shape
    last = strips.shape[0] - 1

    @pl.when(s == 0)
    def _():
        strips[last] = jnp.zeros(strips.shape[1:], BF16)

    lane = lax.broadcasted_iota(jnp.int32, (cl, bw), 1)
    edge = strips[last, :, 0:bw].astype(F32)
    for j in range(some):
        scr[...] = state[:, j].astype(F32)
        slot = s * some + j
        for i in range(bh):
            row = scr[:, i, :]
            edge = jnp.where(lane == slot * 8 + i, row[:, 0:1], edge)
            edge = jnp.where(lane == slot * 8 + 4 + i, row[:, bw - 1 : bw], edge)
            cells = row.astype(BF16)
            rows_out[j, :, i * bw : (i + 1) * bw] = cells
            if i == 0:
                strips[slot, :, 0:bw] = cells
            if i == bh - 1:
                strips[slot, :, bw : 2 * bw] = cells
    strips[last, :, 0:bw] = edge.astype(BF16)


def exchange(rows, strips, tile, below, above, send, recv, own):
    groups = rows.shape[0]
    sec = lax.axis_size("sec")
    tiles = lax.axis_size("tile")
    me = lax.axis_index("chan") * sec + lax.axis_index("sec")
    t = lax.axis_index("tile")
    low, high = t > 0, t < tiles - 1
    mesh = pl.DeviceIdType.MESH

    def at(p):
        return {"chan": p // sec, "sec": lax.rem(p, sec)}

    barrier = pltpu.get_barrier_semaphore()
    for d in range(1, groups):
        pl.semaphore_signal(
            barrier, inc=1, device_id=at(lax.rem(me + d, groups)), device_id_type=mesh
        )

    for step in (1, tiles - 1):
        pl.semaphore_signal(
            barrier, inc=1, device_id={"tile": lax.rem(t + step, tiles)}, device_id_type=mesh
        )
    pl.semaphore_wait(barrier, groups + 1)

    def strip(k, dst, to):
        return pltpu.make_async_remote_copy(
            src_ref=strips, dst_ref=dst, send_sem=send.at[groups + k], recv_sem=recv.at[groups + k],
            device_id={"tile": to}, device_id_type=mesh,
        )

    up, down = strip(0, below, t + 1), strip(1, above, t - 1)

    @pl.when(high)
    def _():
        up.start()

    @pl.when(low)
    def _():
        down.start()

    copies = []
    for d in range(1, groups):
        to = lax.rem(me + d, groups)
        copy = pltpu.make_async_remote_copy(
            src_ref=rows.at[to], dst_ref=tile.at[me], send_sem=send.at[d], recv_sem=recv.at[d],
            device_id=at(to), device_id_type=mesh,
        )
        copy.start()
        copies.append(copy)
    mine = pltpu.make_async_copy(rows.at[me], tile.at[me], own)
    mine.start()
    mine.wait()
    for copy in copies:
        copy.wait()

    @pl.when(high)
    def _():
        up.wait_send()
        down.wait_recv()

    @pl.when(low)
    def _():
        down.wait_send()
        up.wait_recv()


def halo(near, below, mine, above, out, *, per):
    g = pl.program_id(0)
    slots = per * pl.num_programs(0)
    cl = out.shape[2]
    bw = 128
    lane = lax.broadcasted_iota(jnp.int32, (cl, bw), 1)

    def choose(t, m, at):
        got = jnp.where(t == 1, mine[m, :, at].astype(F32), below[m, :, at].astype(F32))
        return jnp.where(t == 2, above[m, :, at].astype(F32), got)

    edge = jnp.zeros((cl, bw), F32)
    for j in range(per):

        def place(k):
            n = near[g * per + j, k]
            m = jnp.maximum(n, 0)
            return n >= 0, m // slots, lax.rem(m, slots)

        for k, lo, unit in ((2, bw, 0), (3, 0, 1)):
            ok, t, m = place(k)
            got = choose(t, m, slice(lo, lo + bw))
            out[0, 2 * j + unit] = jnp.where(ok, got, 0.0).astype(BF16)
        for k, src, dst, count in (
            (4, 7, 0, 1), (0, 4, 1, 4), (6, 4, 5, 1), (5, 3, 6, 1), (1, 0, 7, 4), (7, 0, 11, 1),
        ):
            ok, t, m = place(k)
            to = j * 12 + dst
            turned = pltpu.roll(
                choose(t, slots, slice(0, bw)), lax.rem(to - src - m * 8 + 2 * bw, bw), 1
            )
            here = (lane >= to) & (lane < to + count)
            edge = jnp.where(here, jnp.where(ok, turned, 0.0), edge)
    out[0, 2 * per] = edge.astype(BF16)


def block(tile, rim, pack, out, xs, hid, *, hl):
    groups, _, cl, cells = tile.shape
    chan = groups * cl
    bw = 128
    rows = cells // bw + 2
    s = pl.program_id(0)
    edge = rim[:, rim.shape[1] - 1].reshape(chan, bw).astype(F32)
    edge = pltpu.roll(edge, lax.rem(bw - s * 12, bw), 1)
    lane = lax.broadcasted_iota(jnp.int32, (chan, bw), 1)
    for i in range(rows):
        if i == 0:
            mid = rim[:, 2 * s].reshape(chan, bw)
        elif i == rows - 1:
            mid = rim[:, 2 * s + 1].reshape(chan, bw)
        else:
            mid = tile[:, 0, :, (i - 1) * bw : i * bw].reshape(chan, bw)
        wide = mid.astype(F32)
        left = jnp.where(lane == 0, edge[:, i : i + 1], pltpu.roll(wide, 1, 1))
        right = jnp.where(lane == bw - 1, edge[:, rows + i : rows + i + 1], pltpu.roll(wide, bw - 1, 1))
        at = slice(i * bw, (i + 1) * bw)
        xs[0:chan, at] = left.astype(BF16)
        xs[chan : 2 * chan, at] = mid
        xs[2 * chan : 3 * chan, at] = right.astype(BF16)
    base = 9 * cl
    ident = eye(256, 256)
    cols = [nt(ident, pack[g, base + 2 * hl :, :]) for g in range(groups)]
    bias = jnp.concatenate([c[:cl, 1:2] for c in cols], axis=0)
    gain = jnp.concatenate([c[:cl, 2:3] for c in cols], axis=0)
    acc = jnp.zeros((chan, cells), F32)
    for a in range(3):
        for b in range(3):
            t = 3 * a + b
            w = pack[:, t * cl : (t + 1) * cl, :].reshape(chan, chan)
            acc += jnp.dot(
                w, xs[b * chan : (b + 1) * chan, a * bw : a * bw + cells], preferred_element_type=F32
            )
    acc = acc + bias
    squares = jnp.sum(acc * acc, axis=0, keepdims=True)
    normed = (acc * lax.rsqrt(squares / chan + norm_eps) * gain).astype(BF16)
    for g in range(groups):
        pre = jnp.dot(pack[g, base : base + hl, :], normed, preferred_element_type=F32)
        pre = pre + cols[g][:hl, 0:1]
        act = 0.5 * pre * (1.0 + lax.erf(pre * 0.7071067811865476))
        hid[g * hl : (g + 1) * hl, :] = act.astype(BF16)
    ow = pack[:, base + hl : base + 2 * hl, :].reshape(groups * hl, chan)
    upd = lax.dot_general(ow, hid[...], (((0,), (0,)), ((), ())), preferred_element_type=F32)
    out[:, 0] = upd.astype(BF16).reshape(groups, cl, cells)


def pick(index, table, which, out, wide, got, *, cl):
    s = pl.program_id(0)
    cells = got.shape[0]
    parts = 128 // cl

    @pl.when(s == 0)
    def _():
        wide[...] = table[...].astype(F32)

    def body(j, c):
        for u in range(16):
            at = j * 16 + u
            got[pl.ds(at, 1), :] = wide[pl.ds(index[s * cells + at], 1), :]
        return c

    lax.fori_loop(0, cells // 16, body, 0)
    rows = got[...].astype(BF16)
    part = which[0]
    total = jnp.zeros((cl, cells), F32)
    for k in range(parts):
        total = jnp.where(part == k, nt(eye(cl, 128, k * cl), rows), total)
    out[0] = total.astype(BF16)


def finish(rows, update, force, mask, scale, out, scr):
    cl, some, bh, bw = out.shape
    gain = scale[:, 0:1].astype(F32)
    for j in range(some):
        total = rows[j].astype(F32) + gain * update[j].astype(F32)
        total = (total + force[j].astype(F32)) * mask[j].astype(F32)
        for i in range(bh):
            scr[:, i, :] = total[:, i * bw : (i + 1) * bw]
        out[:, j] = scr[...].astype(BF16)


def on_device(
    ocean_state, atmos, flux_weight, conv_weight, conv_bias, norm_gain, in_weight, in_bias,
    out_weight, layer_scale, cell_mask, neighbours, remap,
):
    cl, slots, bh, bw = ocean_state.shape
    groups = lax.axis_size(("chan", "sec"))
    tiles = lax.axis_size("tile")
    chan = groups * cl
    hl = in_weight.shape[1]
    cells = bh * bw
    per = slots // groups
    some = 4

    state_spec = pl.BlockSpec((cl, some, bh, bw), lambda s, *_: (0, s, 0, 0))
    some_spec = pl.BlockSpec((some, cl, cells), lambda s, *_: (s, 0, 0))
    slot_spec = pl.BlockSpec((1, cl, cells), lambda s, *_: (s, 0, 0))
    rows, strips = pl.pallas_call(
        split_rows,
        grid=(slots // some,),
        in_specs=[state_spec],
        out_specs=[some_spec, whole(slots + 1, cl, 2 * bw)],
        out_shape=[
            jax.ShapeDtypeStruct((slots, cl, cells), BF16),
            jax.ShapeDtypeStruct((slots + 1, cl, 2 * bw), BF16),
        ],
        scratch_shapes=[pltpu.VMEM((cl, bh, bw), F32)],
        compiler_params=params(),
        name="split_rows",
    )(ocean_state)
    vec = jnp.stack(
        [jnp.pad(v, (0, chan - v.shape[0])) for v in (in_bias, conv_bias, norm_gain)]
    )
    vec = jnp.pad(vec, ((0, 13), (0, 0)))
    pack_rows = 9 * cl + 2 * hl + 16
    pack_local = pl.pallas_call(
        pack_weights,
        out_shape=jax.ShapeDtypeStruct((pack_rows, chan), BF16),
        compiler_params=params(),
        name="pack_weights",
    )(jnp.swapaxes(conv_weight, 1, 2), vec, in_weight, out_weight)
    pack = lax.all_gather(pack_local, ("chan", "sec"), axis=0)

    rows, strips, _ = lax.optimization_barrier((rows, strips, pack_local))
    anywhere = pl.BlockSpec(memory_space=pl.ANY)
    tile, below, above = pl.pallas_call(
        exchange,
        in_specs=[anywhere, anywhere],
        out_specs=[anywhere] * 3,
        out_shape=[
            jax.ShapeDtypeStruct((groups, per, cl, cells), BF16),
            jax.ShapeDtypeStruct(strips.shape, BF16),
            jax.ShapeDtypeStruct(strips.shape, BF16),
        ],
        scratch_shapes=[
            pltpu.SemaphoreType.DMA((groups + 2,)),
            pltpu.SemaphoreType.DMA((groups + 2,)),
            pltpu.SemaphoreType.DMA,
        ],
        compiler_params=pltpu.CompilerParams(collective_id=0, has_side_effects=True),
        name="exchange",
    )(rows.reshape(groups, per, cl, cells), strips)
    below, above, atmos = lax.optimization_barrier((below, above, atmos))
    parts = 128 // cl
    trows = atmos.shape[0] // parts
    table = pl.pallas_call(
        flux_rows,
        out_shape=jax.ShapeDtypeStruct((trows, 128), BF16),
        compiler_params=params(),
        name="flux_rows",
    )(atmos, flux_weight.T)
    table = lax.all_gather(table, "tile", axis=0, tiled=True)

    local = lax.rem(remap, trows * parts)
    flat = (remap // (trows * parts)) * trows + lax.rem(local, trows)
    which = (local // trows).reshape(slots, 1, cells)
    lane_spec = pl.BlockSpec((1, 1, cells), lambda s, *_: (s, 0, 0))
    forcing = pl.pallas_call(
        functools.partial(pick, cl=cl),
        grid_spec=pltpu.PrefetchScalarGridSpec(
            num_scalar_prefetch=1,
            grid=(slots,),
            in_specs=[whole(tiles * trows, 128), lane_spec],
            out_specs=slot_spec,
            scratch_shapes=[pltpu.VMEM((tiles * trows, 128), F32), pltpu.VMEM((cells, 128), F32)],
        ),
        out_shape=jax.ShapeDtypeStruct((slots, cl, cells), BF16),
        compiler_params=params(),
        cost_estimate=pl.CostEstimate(flops=10**10, bytes_accessed=4 * 10**6, transcendentals=0),
        name="pick",
    )(flat.reshape(-1), table, which)

    first = (lax.axis_index("tile") - 1) * slots
    near = jnp.where(neighbours >= 0, jnp.clip(neighbours - first, 0, 3 * slots - 1), -1)
    strip_spec = whole(slots + 1, cl, 2 * bw)
    units = 2 * per + 1
    rim = pl.pallas_call(
        functools.partial(halo, per=per),
        grid_spec=pltpu.PrefetchScalarGridSpec(
            num_scalar_prefetch=1,
            grid=(groups,),
            in_specs=[strip_spec, strip_spec, strip_spec],
            out_specs=pl.BlockSpec((1, units, cl, bw), lambda s, *_: (s, 0, 0, 0)),
        ),
        out_shape=jax.ShapeDtypeStruct((groups, units, cl, bw), BF16),
        compiler_params=params(),
        name="halo",
    )(near, below, strips, above)
    rim = lax.all_to_all(rim, ("chan", "sec"), split_axis=0, concat_axis=0)
    update = pl.pallas_call(
        functools.partial(block, hl=hl),
        grid=(per,),
        in_specs=[
            pl.BlockSpec((groups, 1, cl, cells), lambda s: (0, s, 0, 0)),
            whole(groups, units, cl, bw),
            whole(groups, pack_rows, chan),
        ],
        out_specs=pl.BlockSpec((groups, 1, cl, cells), lambda s: (0, s, 0, 0)),
        out_shape=jax.ShapeDtypeStruct((groups, per, cl, cells), BF16),
        scratch_shapes=[
            pltpu.VMEM((3 * chan, (bh + 2) * bw), BF16),
            pltpu.VMEM((groups * hl, cells), BF16),
        ],
        compiler_params=params(),
        name="block",
    )(tile, rim, pack)
    update = lax.all_to_all(update, ("chan", "sec"), split_axis=0, concat_axis=0)
    return pl.pallas_call(
        finish,
        grid=(slots // some,),
        in_specs=[
            some_spec, some_spec, some_spec,
            pl.BlockSpec((some, 1, cells), lambda s: (s, 0, 0)), whole(cl, 1),
        ],
        out_specs=state_spec,
        out_shape=jax.ShapeDtypeStruct(ocean_state.shape, BF16),
        scratch_shapes=[pltpu.VMEM((cl, bh, bw), F32)],
        compiler_params=params(),
        name="finish",
    )(
        rows,
        update.reshape(slots, cl, cells),
        forcing,
        cell_mask.reshape(slots, 1, cells),
        layer_scale.reshape(cl, 1),
    )


def solution(mesh):
    placed = (
        P(("chan", "sec"), ("ens", "tile"), None, None),
        P(("ens", "tile"), None),
        P(None, ("chan", "sec")),
        P(None, None, ("chan", "sec")),
        P(("chan", "sec")),
        P(("chan", "sec")),
        P(None, ("chan", "sec")),
        P(("chan", "sec")),
        P(("chan", "sec"), None),
        P(("chan", "sec")),
        P("tile", None, None),
        P("tile", None),
        P("tile", None, None),
    )
    return jax.shard_map(
        on_device,
        mesh=mesh,
        in_specs=placed,
        out_specs=P(("chan", "sec"), ("ens", "tile"), None, None),
        check_vma=False,
    )
```

```python
import functools

import jax
import jax.numpy as jnp
from jax import lax
from jax.experimental import pallas as pl
from jax.experimental.pallas import tpu as pltpu
from jax.sharding import PartitionSpec as P

norm_eps = 1e-06
F32, BF16 = jnp.float32, jnp.bfloat16
LIMIT = 48 * 1024 * 1024


def params():
    return pltpu.CompilerParams(vmem_limit_bytes=LIMIT)


def nt(a, b):
    return lax.dot_general(a, b, (((1,), (1,)), ((), ())), preferred_element_type=F32)


def whole(*shape):
    return pl.BlockSpec(shape, lambda *_: (0,) * len(shape))


def eye(n, m, off=0):
    r = lax.broadcasted_iota(jnp.int32, (n, m), 0)
    c = lax.broadcasted_iota(jnp.int32, (n, m), 1)
    return jnp.where(c == r + off, 1.0, 0.0).astype(BF16)


def pack_weights(cw, vec, iw, ow, out):
    taps, cl, chan = cw.shape
    hl = iw.shape[1]
    for t in range(taps):
        out[t * cl : (t + 1) * cl, :] = cw[t]
    base = taps * cl
    out[base : base + hl, :] = iw[...].astype(F32).T.astype(BF16)
    out[base + hl : base + 2 * hl, :] = ow[...]
    out[base + 2 * hl :, :] = vec[...]


def flux_rows(atm, fw, out):
    rows = out.shape[0]
    w = fw[...]
    parts = []
    for k in range(atm.shape[0] // rows):
        parts.append(nt(atm[k * rows : (k + 1) * rows, :], w))
    out[...] = jnp.concatenate(parts, axis=1).astype(BF16)


def split_rows(state, rows_out, strips, scr):
    s = pl.program_id(0)
    cl, some, bh, bw = state.shape
    last = strips.shape[0] - 1

    @pl.when(s == 0)
    def _():
        strips[last] = jnp.zeros(strips.shape[1:], BF16)

    lane = lax.broadcasted_iota(jnp.int32, (cl, bw), 1)
    edge = strips[last, :, 0:bw].astype(F32)
    for j in range(some):
        scr[...] = state[:, j].astype(F32)
        slot = s * some + j
        for i in range(bh):
            row = scr[:, i, :]
            edge = jnp.where(lane == slot * 8 + i, row[:, 0:1], edge)
            edge = jnp.where(lane == slot * 8 + 4 + i, row[:, bw - 1 : bw], edge)
            cells = row.astype(BF16)
            rows_out[j, :, i * bw : (i + 1) * bw] = cells
            if i == 0:
                strips[slot, :, 0:bw] = cells
            if i == bh - 1:
                strips[slot, :, bw : 2 * bw] = cells
    strips[last, :, 0:bw] = edge.astype(BF16)


def exchange(rows, strips, pack, tile, below, above, packs, send, recv, wsend, wrecv, own):
    groups = rows.shape[0]
    sec = lax.axis_size("sec")
    tiles = lax.axis_size("tile")
    me = lax.axis_index("chan") * sec + lax.axis_index("sec")
    t = lax.axis_index("tile")
    low, high = t > 0, t < tiles - 1
    mesh = pl.DeviceIdType.MESH

    def at(p):
        return {"chan": p // sec, "sec": lax.rem(p, sec)}

    barrier = pltpu.get_barrier_semaphore()
    for d in range(1, groups):
        pl.semaphore_signal(
            barrier, inc=1, device_id=at(lax.rem(me + d, groups)), device_id_type=mesh
        )

    for step in (1, tiles - 1):
        pl.semaphore_signal(
            barrier, inc=1, device_id={"tile": lax.rem(t + step, tiles)}, device_id_type=mesh
        )
    pl.semaphore_wait(barrier, groups + 1)

    def strip(k, dst, to):
        return pltpu.make_async_remote_copy(
            src_ref=strips, dst_ref=dst, send_sem=send.at[groups + k], recv_sem=recv.at[groups + k],
            device_id={"tile": to}, device_id_type=mesh,
        )

    up, down = strip(0, below, t + 1), strip(1, above, t - 1)

    @pl.when(high)
    def _():
        up.start()

    @pl.when(low)
    def _():
        down.start()

    chans = lax.axis_size("chan")
    c, k = lax.axis_index("chan"), lax.axis_index("sec")

    def weights(src, slot, i, to):
        copy = pltpu.make_async_remote_copy(
            src_ref=src, dst_ref=packs.at[slot], send_sem=wsend.at[i], recv_sem=wrecv.at[i],
            device_id=to, device_id_type=mesh,
        )
        copy.start()
        return copy

    level = [
        weights(pack, me, d, {"chan": lax.rem(c + d, chans)}) for d in range(1, chans)
    ]
    passed = [
        weights(pack, me, e * chans, {"sec": lax.rem(k + e, sec)}) for e in range(1, sec)
    ]
    copies = []
    for d in range(1, groups):
        to = lax.rem(me + d, groups)
        copy = pltpu.make_async_remote_copy(
            src_ref=rows.at[to], dst_ref=tile.at[me], send_sem=send.at[d], recv_sem=recv.at[d],
            device_id=at(to), device_id_type=mesh,
        )
        copy.start()
        copies.append(copy)
    mine = pltpu.make_async_copy(rows.at[me], tile.at[me], own.at[0])
    mine.start()
    held = pltpu.make_async_copy(pack, packs.at[me], own.at[1])
    held.start()
    for d in range(1, chans):
        level[d - 1].wait_recv()
        slot = lax.rem(c - d + chans, chans) * sec + k
        for e in range(1, sec):
            passed.append(
                weights(packs.at[slot], slot, e * chans + d, {"sec": lax.rem(k + e, sec)})
            )
    mine.wait()
    held.wait()
    for copy in level:
        copy.wait_send()
    for copy in passed:
        copy.wait()
    for copy in copies:
        copy.wait()

    @pl.when(high)
    def _():
        up.wait_send()
        down.wait_recv()

    @pl.when(low)
    def _():
        down.wait_send()
        up.wait_recv()


def halo(near, below, mine, above, out, *, per):
    g = pl.program_id(0)
    slots = per * pl.num_programs(0)
    cl = out.shape[2]
    bw = 128
    lane = lax.broadcasted_iota(jnp.int32, (cl, bw), 1)

    def choose(t, m, at):
        got = jnp.where(t == 1, mine[m, :, at].astype(F32), below[m, :, at].astype(F32))
        return jnp.where(t == 2, above[m, :, at].astype(F32), got)

    edge = jnp.zeros((cl, bw), F32)
    for j in range(per):

        def place(k):
            n = near[g * per + j, k]
            m = jnp.maximum(n, 0)
            return n >= 0, m // slots, lax.rem(m, slots)

        for k, lo, unit in ((2, bw, 0), (3, 0, 1)):
            ok, t, m = place(k)
            got = choose(t, m, slice(lo, lo + bw))
            out[0, 2 * j + unit] = jnp.where(ok, got, 0.0).astype(BF16)
        for k, src, dst, count in (
            (4, 7, 0, 1), (0, 4, 1, 4), (6, 4, 5, 1), (5, 3, 6, 1), (1, 0, 7, 4), (7, 0, 11, 1),
        ):
            ok, t, m = place(k)
            to = j * 12 + dst
            turned = pltpu.roll(
                choose(t, slots, slice(0, bw)), lax.rem(to - src - m * 8 + 2 * bw, bw), 1
            )
            here = (lane >= to) & (lane < to + count)
            edge = jnp.where(here, jnp.where(ok, turned, 0.0), edge)
    out[0, 2 * per] = edge.astype(BF16)


def block(tile, rim, pack, out, xs, hid, *, hl):
    groups, _, cl, cells = tile.shape
    chan = groups * cl
    bw = 128
    rows = cells // bw + 2
    s = pl.program_id(0)
    edge = rim[:, rim.shape[1] - 1].reshape(chan, bw).astype(F32)
    edge = pltpu.roll(edge, lax.rem(bw - s * 12, bw), 1)
    lane = lax.broadcasted_iota(jnp.int32, (chan, bw), 1)
    for i in range(rows):
        if i == 0:
            mid = rim[:, 2 * s].reshape(chan, bw)
        elif i == rows - 1:
            mid = rim[:, 2 * s + 1].reshape(chan, bw)
        else:
            mid = tile[:, 0, :, (i - 1) * bw : i * bw].reshape(chan, bw)
        wide = mid.astype(F32)
        left = jnp.where(lane == 0, edge[:, i : i + 1], pltpu.roll(wide, 1, 1))
        right = jnp.where(lane == bw - 1, edge[:, rows + i : rows + i + 1], pltpu.roll(wide, bw - 1, 1))
        at = slice(i * bw, (i + 1) * bw)
        xs[0:chan, at] = left.astype(BF16)
        xs[chan : 2 * chan, at] = mid
        xs[2 * chan : 3 * chan, at] = right.astype(BF16)
    base = 9 * cl
    ident = eye(256, 256)
    cols = [nt(ident, pack[g, base + 2 * hl :, :]) for g in range(groups)]
    bias = jnp.concatenate([c[:cl, 1:2] for c in cols], axis=0)
    gain = jnp.concatenate([c[:cl, 2:3] for c in cols], axis=0)
    acc = jnp.zeros((chan, cells), F32)
    for a in range(3):
        for b in range(3):
            t = 3 * a + b
            w = pack[:, t * cl : (t + 1) * cl, :].reshape(chan, chan)
            acc += jnp.dot(
                w, xs[b * chan : (b + 1) * chan, a * bw : a * bw + cells], preferred_element_type=F32
            )
    acc = acc + bias
    squares = jnp.sum(acc * acc, axis=0, keepdims=True)
    normed = (acc * lax.rsqrt(squares / chan + norm_eps) * gain).astype(BF16)
    for g in range(groups):
        pre = jnp.dot(pack[g, base : base + hl, :], normed, preferred_element_type=F32)
        pre = pre + cols[g][:hl, 0:1]
        act = 0.5 * pre * (1.0 + lax.erf(pre * 0.7071067811865476))
        hid[g * hl : (g + 1) * hl, :] = act.astype(BF16)
    ow = pack[:, base + hl : base + 2 * hl, :].reshape(groups * hl, chan)
    upd = lax.dot_general(ow, hid[...], (((0,), (0,)), ((), ())), preferred_element_type=F32)
    out[:, 0] = upd.astype(BF16).reshape(groups, cl, cells)


def pick(index, table, which, out, wide, got, *, cl):
    s = pl.program_id(0)
    cells = got.shape[0]
    parts = 128 // cl

    @pl.when(s == 0)
    def _():
        wide[...] = table[...].astype(F32)

    def body(j, c):
        for u in range(16):
            at = j * 16 + u
            got[pl.ds(at, 1), :] = wide[pl.ds(index[s * cells + at], 1), :]
        return c

    lax.fori_loop(0, cells // 16, body, 0)
    rows = got[...].astype(BF16)
    part = which[0]
    total = jnp.zeros((cl, cells), F32)
    for k in range(parts):
        total = jnp.where(part == k, nt(eye(cl, 128, k * cl), rows), total)
    out[0] = total.astype(BF16)


def finish(rows, update, early, late, mask, scale, out, scr):
    cl, some, bh, bw = out.shape
    gain = scale[:, 0:1].astype(F32)
    first = pl.program_id(0) < pl.num_programs(0) // 2
    for j in range(some):
        total = rows[j].astype(F32) + gain * update[j].astype(F32)
        force = jnp.where(first, early[j].astype(F32), late[j].astype(F32))
        total = (total + force) * mask[j].astype(F32)
        for i in range(bh):
            scr[:, i, :] = total[:, i * bw : (i + 1) * bw]
        out[:, j] = scr[...].astype(BF16)


def on_device(
    ocean_state, atmos, flux_weight, conv_weight, conv_bias, norm_gain, in_weight, in_bias,
    out_weight, layer_scale, cell_mask, neighbours, remap,
):
    cl, slots, bh, bw = ocean_state.shape
    groups = lax.axis_size(("chan", "sec"))
    tiles = lax.axis_size("tile")
    chan = groups * cl
    hl = in_weight.shape[1]
    cells = bh * bw
    per = slots // groups
    some = 4

    state_spec = pl.BlockSpec((cl, some, bh, bw), lambda s, *_: (0, s, 0, 0))
    some_spec = pl.BlockSpec((some, cl, cells), lambda s, *_: (s, 0, 0))
    slot_spec = pl.BlockSpec((1, cl, cells), lambda s, *_: (s, 0, 0))
    rows, strips = pl.pallas_call(
        split_rows,
        grid=(slots // some,),
        in_specs=[state_spec],
        out_specs=[some_spec, whole(slots + 1, cl, 2 * bw)],
        out_shape=[
            jax.ShapeDtypeStruct((slots, cl, cells), BF16),
            jax.ShapeDtypeStruct((slots + 1, cl, 2 * bw), BF16),
        ],
        scratch_shapes=[pltpu.VMEM((cl, bh, bw), F32)],
        compiler_params=params(),
        name="split_rows",
    )(ocean_state)
    vec = jnp.stack(
        [jnp.pad(v, (0, chan - v.shape[0])) for v in (in_bias, conv_bias, norm_gain)]
    )
    vec = jnp.pad(vec, ((0, 13), (0, 0)))
    pack_rows = 9 * cl + 2 * hl + 16
    pack_local = pl.pallas_call(
        pack_weights,
        out_shape=jax.ShapeDtypeStruct((pack_rows, chan), BF16),
        compiler_params=params(),
        name="pack_weights",
    )(jnp.swapaxes(conv_weight, 1, 2), vec, in_weight, out_weight)

    parts = 128 // cl
    trows = atmos.shape[0] // parts
    table = pl.pallas_call(
        flux_rows,
        out_shape=jax.ShapeDtypeStruct((trows, 128), BF16),
        compiler_params=params(),
        name="flux_rows",
    )(atmos, flux_weight.T)
    rows, strips, pack_local, table = lax.optimization_barrier((rows, strips, pack_local, table))
    table = lax.all_gather(table, "tile", axis=0, tiled=True)

    anywhere = pl.BlockSpec(memory_space=pl.ANY)
    tile, below, above, pack = pl.pallas_call(
        exchange,
        in_specs=[anywhere] * 3,
        out_specs=[anywhere] * 4,
        out_shape=[
            jax.ShapeDtypeStruct((groups, per, cl, cells), BF16),
            jax.ShapeDtypeStruct(strips.shape, BF16),
            jax.ShapeDtypeStruct(strips.shape, BF16),
            jax.ShapeDtypeStruct((groups, pack_rows, chan), BF16),
        ],
        scratch_shapes=[
            pltpu.SemaphoreType.DMA((groups + 2,)),
            pltpu.SemaphoreType.DMA((groups + 2,)),
            pltpu.SemaphoreType.DMA((groups,)),
            pltpu.SemaphoreType.DMA((groups,)),
            pltpu.SemaphoreType.DMA((2,)),
        ],
        compiler_params=pltpu.CompilerParams(collective_id=0, has_side_effects=True),
        name="exchange",
    )(rows.reshape(groups, per, cl, cells), strips, pack_local)
    local = lax.rem(remap, trows * parts)
    flat = (remap // (trows * parts)) * trows + lax.rem(local, trows)
    which = (local // trows).reshape(slots, 1, cells)
    lane_spec = pl.BlockSpec((1, 1, cells), lambda s, *_: (s, 0, 0))
    picks = pl.pallas_call(
        functools.partial(pick, cl=cl),
        grid_spec=pltpu.PrefetchScalarGridSpec(
            num_scalar_prefetch=1,
            grid=(slots // 2,),
            in_specs=[whole(tiles * trows, 128), lane_spec],
            out_specs=slot_spec,
            scratch_shapes=[pltpu.VMEM((tiles * trows, 128), F32), pltpu.VMEM((cells, 128), F32)],
        ),
        out_shape=jax.ShapeDtypeStruct((slots // 2, cl, cells), BF16),
        compiler_params=params(),
        cost_estimate=pl.CostEstimate(flops=5 * 10**9, bytes_accessed=4 * 10**6, transcendentals=0),
        name="pick",
    )
    flat, half = flat.reshape(2, -1), slots // 2

    first = (lax.axis_index("tile") - 1) * slots
    near = jnp.where(neighbours >= 0, jnp.clip(neighbours - first, 0, 3 * slots - 1), -1)
    strip_spec = whole(slots + 1, cl, 2 * bw)
    units = 2 * per + 1
    rim = pl.pallas_call(
        functools.partial(halo, per=per),
        grid_spec=pltpu.PrefetchScalarGridSpec(
            num_scalar_prefetch=1,
            grid=(groups,),
            in_specs=[strip_spec, strip_spec, strip_spec],
            out_specs=pl.BlockSpec((1, units, cl, bw), lambda s, *_: (s, 0, 0, 0)),
        ),
        out_shape=jax.ShapeDtypeStruct((groups, units, cl, bw), BF16),
        compiler_params=params(),
        name="halo",
    )(near, below, strips, above)
    early, rim = lax.optimization_barrier((flat[0], rim))
    early = picks(early, table, which[:half])
    rim = lax.all_to_all(rim, ("chan", "sec"), split_axis=0, concat_axis=0)
    early, tile = lax.optimization_barrier((early, tile))
    update = pl.pallas_call(
        functools.partial(block, hl=hl),
        grid=(per,),
        in_specs=[
            pl.BlockSpec((groups, 1, cl, cells), lambda s: (0, s, 0, 0)),
            whole(groups, units, cl, bw),
            whole(groups, pack_rows, chan),
        ],
        out_specs=pl.BlockSpec((groups, 1, cl, cells), lambda s: (0, s, 0, 0)),
        out_shape=jax.ShapeDtypeStruct((groups, per, cl, cells), BF16),
        scratch_shapes=[
            pltpu.VMEM((3 * chan, (bh + 2) * bw), BF16),
            pltpu.VMEM((groups * hl, cells), BF16),
        ],
        compiler_params=params(),
        name="block",
    )(tile, rim, pack)
    late, update = lax.optimization_barrier((flat[1], update))
    late = picks(late, table, which[half:])
    update = lax.all_to_all(update, ("chan", "sec"), split_axis=0, concat_axis=0)
    last = half // some - 1
    return pl.pallas_call(
        finish,
        grid=(slots // some,),
        in_specs=[
            some_spec, some_spec,
            pl.BlockSpec((some, cl, cells), lambda s: (jnp.minimum(s, last), 0, 0)),
            pl.BlockSpec((some, cl, cells), lambda s: (jnp.maximum(s - last - 1, 0), 0, 0)),
            pl.BlockSpec((some, 1, cells), lambda s: (s, 0, 0)), whole(cl, 1),
        ],
        out_specs=state_spec,
        out_shape=jax.ShapeDtypeStruct(ocean_state.shape, BF16),
        scratch_shapes=[pltpu.VMEM((cl, bh, bw), F32)],
        compiler_params=params(),
        name="finish",
    )(
        rows,
        update.reshape(slots, cl, cells),
        early,
        late,
        cell_mask.reshape(slots, 1, cells),
        layer_scale.reshape(cl, 1),
    )


def solution(mesh):
    placed = (
        P(("chan", "sec"), ("ens", "tile"), None, None),
        P(("ens", "tile"), None),
        P(None, ("chan", "sec")),
        P(None, None, ("chan", "sec")),
        P(("chan", "sec")),
        P(("chan", "sec")),
        P(None, ("chan", "sec")),
        P(("chan", "sec")),
        P(("chan", "sec"), None),
        P(("chan", "sec")),
        P("tile", None, None),
        P("tile", None),
        P("tile", None, None),
    )
    return jax.shard_map(
        on_device,
        mesh=mesh,
        in_specs=placed,
        out_specs=P(("chan", "sec"), ("ens", "tile"), None, None),
        check_vma=False,
    )
```

```python
import functools

import jax
import jax.numpy as jnp
from jax import lax
from jax.experimental import pallas as pl
from jax.experimental.pallas import tpu as pltpu
from jax.sharding import PartitionSpec as P

norm_eps = 1e-06
F32, BF16 = jnp.float32, jnp.bfloat16
LIMIT = 48 * 1024 * 1024


def params():
    return pltpu.CompilerParams(vmem_limit_bytes=LIMIT)


def nt(a, b):
    return lax.dot_general(a, b, (((1,), (1,)), ((), ())), preferred_element_type=F32)


def whole(*shape):
    return pl.BlockSpec(shape, lambda *_: (0,) * len(shape))


def eye(n, m, off=0):
    r = lax.broadcasted_iota(jnp.int32, (n, m), 0)
    c = lax.broadcasted_iota(jnp.int32, (n, m), 1)
    return jnp.where(c == r + off, 1.0, 0.0).astype(BF16)


def pack_weights(cw, vec, iw, ow, out):
    taps, cl, chan = cw.shape
    hl = iw.shape[1]
    for t in range(taps):
        out[t * cl : (t + 1) * cl, :] = cw[t]
    base = taps * cl
    out[base : base + hl, :] = iw[...].astype(F32).T.astype(BF16)
    out[base + hl : base + 2 * hl, :] = ow[...]
    out[base + 2 * hl :, :] = vec[...]


def flux_rows(atm, fw, out):
    rows = out.shape[0]
    w = fw[...]
    parts = []
    for k in range(atm.shape[0] // rows):
        parts.append(nt(atm[k * rows : (k + 1) * rows, :], w))
    out[...] = jnp.concatenate(parts, axis=1).astype(BF16)


def split_rows(state, rows_out, strips, scr):
    s = pl.program_id(0)
    cl, some, bh, bw = state.shape
    last = strips.shape[0] - 1

    @pl.when(s == 0)
    def _():
        strips[last] = jnp.zeros(strips.shape[1:], BF16)

    lane = lax.broadcasted_iota(jnp.int32, (cl, bw), 1)
    edge = strips[last, :, 0:bw].astype(F32)
    for j in range(some):
        scr[...] = state[:, j].astype(F32)
        slot = s * some + j
        for i in range(bh):
            row = scr[:, i, :]
            edge = jnp.where(lane == slot * 8 + i, row[:, 0:1], edge)
            edge = jnp.where(lane == slot * 8 + 4 + i, row[:, bw - 1 : bw], edge)
            cells = row.astype(BF16)
            rows_out[j, :, i * bw : (i + 1) * bw] = cells
            if i == 0:
                strips[slot, :, 0:bw] = cells
            if i == bh - 1:
                strips[slot, :, bw : 2 * bw] = cells
    strips[last, :, 0:bw] = edge.astype(BF16)


def exchange(rows, strips, pack, tile, below, above, packs, send, recv, wsend, wrecv, own):
    groups = rows.shape[0]
    sec = lax.axis_size("sec")
    tiles = lax.axis_size("tile")
    me = lax.axis_index("chan") * sec + lax.axis_index("sec")
    t = lax.axis_index("tile")
    low, high = t > 0, t < tiles - 1
    mesh = pl.DeviceIdType.MESH

    def at(p):
        return {"chan": p // sec, "sec": lax.rem(p, sec)}

    barrier = pltpu.get_barrier_semaphore()
    for d in range(1, groups):
        pl.semaphore_signal(
            barrier, inc=1, device_id=at(lax.rem(me + d, groups)), device_id_type=mesh
        )

    for step in (1, tiles - 1):
        pl.semaphore_signal(
            barrier, inc=1, device_id={"tile": lax.rem(t + step, tiles)}, device_id_type=mesh
        )
    pl.semaphore_wait(barrier, groups + 1)

    def strip(k, dst, to):
        return pltpu.make_async_remote_copy(
            src_ref=strips, dst_ref=dst, send_sem=send.at[groups + k], recv_sem=recv.at[groups + k],
            device_id={"tile": to}, device_id_type=mesh,
        )

    up, down = strip(0, below, t + 1), strip(1, above, t - 1)

    @pl.when(high)
    def _():
        up.start()

    @pl.when(low)
    def _():
        down.start()

    chans = lax.axis_size("chan")
    c, k = lax.axis_index("chan"), lax.axis_index("sec")

    def weights(src, slot, i, to):
        copy = pltpu.make_async_remote_copy(
            src_ref=src, dst_ref=packs.at[slot], send_sem=wsend.at[i], recv_sem=wrecv.at[i],
            device_id=to, device_id_type=mesh,
        )
        copy.start()
        return copy

    level = [
        weights(pack, me, d, {"chan": lax.rem(c + d, chans)}) for d in range(1, chans)
    ]
    passed = [
        weights(pack, me, e * chans, {"sec": lax.rem(k + e, sec)}) for e in range(1, sec)
    ]
    copies = []
    for d in range(1, groups):
        to = lax.rem(me + d, groups)
        copy = pltpu.make_async_remote_copy(
            src_ref=rows.at[to], dst_ref=tile.at[me], send_sem=send.at[d], recv_sem=recv.at[d],
            device_id=at(to), device_id_type=mesh,
        )
        copy.start()
        copies.append(copy)
    mine = pltpu.make_async_copy(rows.at[me], tile.at[me], own.at[0])
    mine.start()
    held = pltpu.make_async_copy(pack, packs.at[me], own.at[1])
    held.start()
    for d in range(1, chans):
        level[d - 1].wait_recv()
        slot = lax.rem(c - d + chans, chans) * sec + k
        for e in range(1, sec):
            passed.append(
                weights(packs.at[slot], slot, e * chans + d, {"sec": lax.rem(k + e, sec)})
            )
    mine.wait()
    held.wait()
    for copy in level:
        copy.wait_send()
    for copy in passed:
        copy.wait()
    for copy in copies:
        copy.wait()

    @pl.when(high)
    def _():
        up.wait_send()
        down.wait_recv()

    @pl.when(low)
    def _():
        down.wait_send()
        up.wait_recv()


def halo(near, below, mine, above, out, *, per):
    g = pl.program_id(0)
    slots = per * pl.num_programs(0)
    cl = out.shape[2]
    bw = 128
    lane = lax.broadcasted_iota(jnp.int32, (cl, bw), 1)

    def choose(t, m, at):
        got = jnp.where(t == 1, mine[m, :, at].astype(F32), below[m, :, at].astype(F32))
        return jnp.where(t == 2, above[m, :, at].astype(F32), got)

    edge = jnp.zeros((cl, bw), F32)
    for j in range(per):

        def place(k):
            n = near[g * per + j, k]
            m = jnp.maximum(n, 0)
            return n >= 0, m // slots, lax.rem(m, slots)

        for k, lo, unit in ((2, bw, 0), (3, 0, 1)):
            ok, t, m = place(k)
            got = choose(t, m, slice(lo, lo + bw))
            out[0, 2 * j + unit] = jnp.where(ok, got, 0.0).astype(BF16)
        for k, src, dst, count in (
            (4, 7, 0, 1), (0, 4, 1, 4), (6, 4, 5, 1), (5, 3, 6, 1), (1, 0, 7, 4), (7, 0, 11, 1),
        ):
            ok, t, m = place(k)
            to = j * 12 + dst
            turned = pltpu.roll(
                choose(t, slots, slice(0, bw)), lax.rem(to - src - m * 8 + 2 * bw, bw), 1
            )
            here = (lane >= to) & (lane < to + count)
            edge = jnp.where(here, jnp.where(ok, turned, 0.0), edge)
    out[0, 2 * per] = edge.astype(BF16)


def block(tile, rim, pack, out, xs, hid, *, hl):
    groups, _, cl, cells = tile.shape
    chan = groups * cl
    bw = 128
    rows = cells // bw + 2
    s = pl.program_id(0)
    edge = rim[:, rim.shape[1] - 1].reshape(chan, bw).astype(F32)
    edge = pltpu.roll(edge, lax.rem(bw - s * 12, bw), 1)
    lane = lax.broadcasted_iota(jnp.int32, (chan, bw), 1)
    for i in range(rows):
        if i == 0:
            mid = rim[:, 2 * s].reshape(chan, bw)
        elif i == rows - 1:
            mid = rim[:, 2 * s + 1].reshape(chan, bw)
        else:
            mid = tile[:, 0, :, (i - 1) * bw : i * bw].reshape(chan, bw)
        wide = mid.astype(F32)
        left = jnp.where(lane == 0, edge[:, i : i + 1], pltpu.roll(wide, 1, 1))
        right = jnp.where(lane == bw - 1, edge[:, rows + i : rows + i + 1], pltpu.roll(wide, bw - 1, 1))
        at = slice(i * bw, (i + 1) * bw)
        xs[0:chan, at] = left.astype(BF16)
        xs[chan : 2 * chan, at] = mid
        xs[2 * chan : 3 * chan, at] = right.astype(BF16)
    base = 9 * cl
    ident = eye(256, 256)
    cols = [nt(ident, pack[g, base + 2 * hl :, :]) for g in range(groups)]
    bias = jnp.concatenate([c[:cl, 1:2] for c in cols], axis=0)
    gain = jnp.concatenate([c[:cl, 2:3] for c in cols], axis=0)
    acc = jnp.zeros((chan, cells), F32)
    for a in range(3):
        for b in range(3):
            t = 3 * a + b
            w = pack[:, t * cl : (t + 1) * cl, :].reshape(chan, chan)
            acc += jnp.dot(
                w, xs[b * chan : (b + 1) * chan, a * bw : a * bw + cells], preferred_element_type=F32
            )
    acc = acc + bias
    squares = jnp.sum(acc * acc, axis=0, keepdims=True)
    normed = (acc * lax.rsqrt(squares / chan + norm_eps) * gain).astype(BF16)
    for g in range(groups):
        pre = jnp.dot(pack[g, base : base + hl, :], normed, preferred_element_type=F32)
        pre = pre + cols[g][:hl, 0:1]
        act = 0.5 * pre * (1.0 + lax.erf(pre * 0.7071067811865476))
        hid[g * hl : (g + 1) * hl, :] = act.astype(BF16)
    ow = pack[:, base + hl : base + 2 * hl, :].reshape(groups * hl, chan)
    upd = lax.dot_general(ow, hid[...], (((0,), (0,)), ((), ())), preferred_element_type=F32)
    out[:, 0] = upd.astype(BF16).reshape(groups, cl, cells)


def pick(index, table, which, out, wide, got, *, cl):
    s = pl.program_id(0)
    cells = got.shape[0]
    parts = 128 // cl

    @pl.when(s == 0)
    def _():
        wide[...] = table[...].astype(F32)

    def body(j, c):
        for u in range(16):
            at = j * 16 + u
            got[pl.ds(at, 1), :] = wide[pl.ds(index[s * cells + at], 1), :]
        return c

    lax.fori_loop(0, cells // 16, body, 0)
    rows = got[...].astype(BF16)
    part = which[0]
    total = jnp.zeros((cl, cells), F32)
    for k in range(parts):
        total = jnp.where(part == k, nt(eye(cl, 128, k * cl), rows), total)
    out[0] = total.astype(BF16)


def finish(rows, update, force, mask, scale, out, scr):
    cl, some, bh, bw = out.shape
    gain = scale[:, 0:1].astype(F32)
    for j in range(some):
        total = rows[j].astype(F32) + gain * update[j].astype(F32)
        total = (total + force[j].astype(F32)) * mask[j].astype(F32)
        for i in range(bh):
            scr[:, i, :] = total[:, i * bw : (i + 1) * bw]
        out[:, j] = scr[...].astype(BF16)


def on_device(
    ocean_state, atmos, flux_weight, conv_weight, conv_bias, norm_gain, in_weight, in_bias,
    out_weight, layer_scale, cell_mask, neighbours, remap,
):
    cl, slots, bh, bw = ocean_state.shape
    groups = lax.axis_size(("chan", "sec"))
    tiles = lax.axis_size("tile")
    chan = groups * cl
    hl = in_weight.shape[1]
    cells = bh * bw
    per = slots // groups
    some = 4

    state_spec = pl.BlockSpec((cl, some, bh, bw), lambda s, *_: (0, s, 0, 0))
    some_spec = pl.BlockSpec((some, cl, cells), lambda s, *_: (s, 0, 0))
    slot_spec = pl.BlockSpec((1, cl, cells), lambda s, *_: (s, 0, 0))
    rows, strips = pl.pallas_call(
        split_rows,
        grid=(slots // some,),
        in_specs=[state_spec],
        out_specs=[some_spec, whole(slots + 1, cl, 2 * bw)],
        out_shape=[
            jax.ShapeDtypeStruct((slots, cl, cells), BF16),
            jax.ShapeDtypeStruct((slots + 1, cl, 2 * bw), BF16),
        ],
        scratch_shapes=[pltpu.VMEM((cl, bh, bw), F32)],
        compiler_params=params(),
        name="split_rows",
    )(ocean_state)
    vec = jnp.stack(
        [jnp.pad(v, (0, chan - v.shape[0])) for v in (in_bias, conv_bias, norm_gain)]
    )
    vec = jnp.pad(vec, ((0, 13), (0, 0)))
    pack_rows = 9 * cl + 2 * hl + 16
    pack_local = pl.pallas_call(
        pack_weights,
        out_shape=jax.ShapeDtypeStruct((pack_rows, chan), BF16),
        compiler_params=params(),
        name="pack_weights",
    )(jnp.swapaxes(conv_weight, 1, 2), vec, in_weight, out_weight)

    parts = 128 // cl
    trows = atmos.shape[0] // parts
    table = pl.pallas_call(
        flux_rows,
        out_shape=jax.ShapeDtypeStruct((trows, 128), BF16),
        compiler_params=params(),
        name="flux_rows",
    )(atmos, flux_weight.T)
    rows, strips, pack_local, table = lax.optimization_barrier((rows, strips, pack_local, table))

    resident = pl.BlockSpec(memory_space=pltpu.VMEM)
    tile, below, above, pack = pl.pallas_call(
        exchange,
        in_specs=[resident] * 3,
        out_specs=[resident] * 4,
        out_shape=[
            jax.ShapeDtypeStruct((groups, per, cl, cells), BF16),
            jax.ShapeDtypeStruct(strips.shape, BF16),
            jax.ShapeDtypeStruct(strips.shape, BF16),
            jax.ShapeDtypeStruct((groups, pack_rows, chan), BF16),
        ],
        scratch_shapes=[
            pltpu.SemaphoreType.DMA((groups + 2,)),
            pltpu.SemaphoreType.DMA((groups + 2,)),
            pltpu.SemaphoreType.DMA((groups,)),
            pltpu.SemaphoreType.DMA((groups,)),
            pltpu.SemaphoreType.DMA((2,)),
        ],
        compiler_params=pltpu.CompilerParams(
            collective_id=0, has_side_effects=True, vmem_limit_bytes=LIMIT
        ),
        name="exchange",
    )(rows.reshape(groups, per, cl, cells), strips, pack_local)
    below, above, table = lax.optimization_barrier((below, above, table))
    table = lax.all_gather(table, "tile", axis=0, tiled=True)
    local = lax.rem(remap, trows * parts)
    flat = (remap // (trows * parts)) * trows + lax.rem(local, trows)
    which = (local // trows).reshape(slots, 1, cells)
    lane_spec = pl.BlockSpec((1, 1, cells), lambda s, *_: (s, 0, 0))
    picks = pl.pallas_call(
        functools.partial(pick, cl=cl),
        grid_spec=pltpu.PrefetchScalarGridSpec(
            num_scalar_prefetch=1,
            grid=(slots,),
            in_specs=[whole(tiles * trows, 128), lane_spec],
            out_specs=slot_spec,
            scratch_shapes=[pltpu.VMEM((tiles * trows, 128), F32), pltpu.VMEM((cells, 128), F32)],
        ),
        out_shape=jax.ShapeDtypeStruct((slots, cl, cells), BF16),
        compiler_params=params(),
        cost_estimate=pl.CostEstimate(flops=10**10, bytes_accessed=4 * 10**6, transcendentals=0),
        name="pick",
    )
    flat = flat.reshape(-1)

    first = (lax.axis_index("tile") - 1) * slots
    near = jnp.where(neighbours >= 0, jnp.clip(neighbours - first, 0, 3 * slots - 1), -1)
    strip_spec = whole(slots + 1, cl, 2 * bw)
    units = 2 * per + 1
    rim = pl.pallas_call(
        functools.partial(halo, per=per),
        grid_spec=pltpu.PrefetchScalarGridSpec(
            num_scalar_prefetch=1,
            grid=(groups,),
            in_specs=[strip_spec, strip_spec, strip_spec],
            out_specs=pl.BlockSpec((1, units, cl, bw), lambda s, *_: (s, 0, 0, 0)),
        ),
        out_shape=jax.ShapeDtypeStruct((groups, units, cl, bw), BF16),
        compiler_params=params(),
        name="halo",
    )(near, below, strips, above)
    rim = lax.all_to_all(rim, ("chan", "sec"), split_axis=0, concat_axis=0)
    update = pl.pallas_call(
        functools.partial(block, hl=hl),
        grid=(per,),
        in_specs=[
            pl.BlockSpec((groups, 1, cl, cells), lambda s: (0, s, 0, 0)),
            whole(groups, units, cl, bw),
            whole(groups, pack_rows, chan),
        ],
        out_specs=pl.BlockSpec((groups, 1, cl, cells), lambda s: (0, s, 0, 0)),
        out_shape=jax.ShapeDtypeStruct((groups, per, cl, cells), BF16),
        scratch_shapes=[
            pltpu.VMEM((3 * chan, (bh + 2) * bw), BF16),
            pltpu.VMEM((groups * hl, cells), BF16),
        ],
        compiler_params=params(),
        name="block",
    )(tile, rim, pack)
    flat, update = lax.optimization_barrier((flat, update))
    forcing = picks(flat, table, which)
    update = lax.all_to_all(update, ("chan", "sec"), split_axis=0, concat_axis=0)
    return pl.pallas_call(
        finish,
        grid=(slots // some,),
        in_specs=[
            some_spec, some_spec, some_spec,
            pl.BlockSpec((some, 1, cells), lambda s: (s, 0, 0)), whole(cl, 1),
        ],
        out_specs=state_spec,
        out_shape=jax.ShapeDtypeStruct(ocean_state.shape, BF16),
        scratch_shapes=[pltpu.VMEM((cl, bh, bw), F32)],
        compiler_params=params(),
        name="finish",
    )(
        rows,
        update.reshape(slots, cl, cells),
        forcing,
        cell_mask.reshape(slots, 1, cells),
        layer_scale.reshape(cl, 1),
    )


def solution(mesh):
    placed = (
        P(("chan", "sec"), ("ens", "tile"), None, None),
        P(("ens", "tile"), None),
        P(None, ("chan", "sec")),
        P(None, None, ("chan", "sec")),
        P(("chan", "sec")),
        P(("chan", "sec")),
        P(None, ("chan", "sec")),
        P(("chan", "sec")),
        P(("chan", "sec"), None),
        P(("chan", "sec")),
        P("tile", None, None),
        P("tile", None),
        P("tile", None, None),
    )
    return jax.shard_map(
        on_device,
        mesh=mesh,
        in_specs=placed,
        out_specs=P(("chan", "sec"), ("ens", "tile"), None, None),
        check_vma=False,
    )
```

```python
import functools

import jax
import jax.numpy as jnp
from jax import lax
from jax.experimental import pallas as pl
from jax.experimental.pallas import tpu as pltpu
from jax.sharding import PartitionSpec as P

norm_eps = 1e-06
F32, BF16 = jnp.float32, jnp.bfloat16
LIMIT = 48 * 1024 * 1024


def params():
    return pltpu.CompilerParams(vmem_limit_bytes=LIMIT)


def nt(a, b):
    return lax.dot_general(a, b, (((1,), (1,)), ((), ())), preferred_element_type=F32)


def whole(*shape):
    return pl.BlockSpec(shape, lambda *_: (0,) * len(shape))


def eye(n, m, off=0):
    r = lax.broadcasted_iota(jnp.int32, (n, m), 0)
    c = lax.broadcasted_iota(jnp.int32, (n, m), 1)
    return jnp.where(c == r + off, 1.0, 0.0).astype(BF16)


def pack_weights(cw, vec, iw, ow, out):
    taps, cl, chan = cw.shape
    hl = iw.shape[1]
    for t in range(taps):
        out[t * cl : (t + 1) * cl, :] = cw[t]
    base = taps * cl
    out[base : base + hl, :] = iw[...].astype(F32).T.astype(BF16)
    out[base + hl : base + 2 * hl, :] = ow[...]
    out[base + 2 * hl :, :] = vec[...]


def flux_rows(atm, fw, out):
    rows = out.shape[0]
    w = fw[...]
    parts = []
    for k in range(atm.shape[0] // rows):
        parts.append(nt(atm[k * rows : (k + 1) * rows, :], w))
    out[...] = jnp.concatenate(parts, axis=1).astype(BF16)


def split_rows(state, rows_out, strips, scr):
    s = pl.program_id(0)
    cl, some, bh, bw = state.shape
    last = strips.shape[0] - 1

    @pl.when(s == 0)
    def _():
        strips[last] = jnp.zeros(strips.shape[1:], BF16)

    lane = lax.broadcasted_iota(jnp.int32, (cl, bw), 1)
    edge = strips[last, :, 0:bw].astype(F32)
    for j in range(some):
        scr[...] = state[:, j].astype(F32)
        slot = s * some + j
        for i in range(bh):
            row = scr[:, i, :]
            edge = jnp.where(lane == slot * 8 + i, row[:, 0:1], edge)
            edge = jnp.where(lane == slot * 8 + 4 + i, row[:, bw - 1 : bw], edge)
            cells = row.astype(BF16)
            rows_out[j, :, i * bw : (i + 1) * bw] = cells
            if i == 0:
                strips[slot, :, 0:bw] = cells
            if i == bh - 1:
                strips[slot, :, bw : 2 * bw] = cells
    strips[last, :, 0:bw] = edge.astype(BF16)


def exchange(rows, strips, tile, below, above, send, recv, own):
    groups = rows.shape[0]
    sec = lax.axis_size("sec")
    tiles = lax.axis_size("tile")
    me = lax.axis_index("chan") * sec + lax.axis_index("sec")
    t = lax.axis_index("tile")
    low, high = t > 0, t < tiles - 1
    mesh = pl.DeviceIdType.MESH

    def at(p):
        return {"chan": p // sec, "sec": lax.rem(p, sec)}

    barrier = pltpu.get_barrier_semaphore()
    for d in range(1, groups):
        pl.semaphore_signal(
            barrier, inc=1, device_id=at(lax.rem(me + d, groups)), device_id_type=mesh
        )

    for step in (1, tiles - 1):
        pl.semaphore_signal(
            barrier, inc=1, device_id={"tile": lax.rem(t + step, tiles)}, device_id_type=mesh
        )
    pl.semaphore_wait(barrier, groups + 1)

    def strip(k, dst, to):
        return pltpu.make_async_remote_copy(
            src_ref=strips, dst_ref=dst, send_sem=send.at[groups + k], recv_sem=recv.at[groups + k],
            device_id={"tile": to}, device_id_type=mesh,
        )

    up, down = strip(0, below, t + 1), strip(1, above, t - 1)

    @pl.when(high)
    def _():
        up.start()

    @pl.when(low)
    def _():
        down.start()

    copies = []
    for d in range(1, groups):
        to = lax.rem(me + d, groups)
        copy = pltpu.make_async_remote_copy(
            src_ref=rows.at[to], dst_ref=tile.at[me], send_sem=send.at[d], recv_sem=recv.at[d],
            device_id=at(to), device_id_type=mesh,
        )
        copy.start()
        copies.append(copy)
    mine = pltpu.make_async_copy(rows.at[me], tile.at[me], own)
    mine.start()
    mine.wait()
    for copy in copies:
        copy.wait()

    @pl.when(high)
    def _():
        up.wait_send()
        down.wait_recv()

    @pl.when(low)
    def _():
        down.wait_send()
        up.wait_recv()


def halo(near, below, mine, above, out, *, per):
    g = pl.program_id(0)
    slots = per * pl.num_programs(0)
    cl = out.shape[2]
    bw = 128
    lane = lax.broadcasted_iota(jnp.int32, (cl, bw), 1)

    def choose(t, m, at):
        got = jnp.where(t == 1, mine[m, :, at].astype(F32), below[m, :, at].astype(F32))
        return jnp.where(t == 2, above[m, :, at].astype(F32), got)

    edge = jnp.zeros((cl, bw), F32)
    for j in range(per):

        def place(k):
            n = near[g * per + j, k]
            m = jnp.maximum(n, 0)
            return n >= 0, m // slots, lax.rem(m, slots)

        for k, lo, unit in ((2, bw, 0), (3, 0, 1)):
            ok, t, m = place(k)
            got = choose(t, m, slice(lo, lo + bw))
            out[0, 2 * j + unit] = jnp.where(ok, got, 0.0).astype(BF16)
        for k, src, dst, count in (
            (4, 7, 0, 1), (0, 4, 1, 4), (6, 4, 5, 1), (5, 3, 6, 1), (1, 0, 7, 4), (7, 0, 11, 1),
        ):
            ok, t, m = place(k)
            to = j * 12 + dst
            turned = pltpu.roll(
                choose(t, slots, slice(0, bw)), lax.rem(to - src - m * 8 + 2 * bw, bw), 1
            )
            here = (lane >= to) & (lane < to + count)
            edge = jnp.where(here, jnp.where(ok, turned, 0.0), edge)
    out[0, 2 * per] = edge.astype(BF16)


def block(tile, rim, pack, out, xs, hid, *, hl):
    groups, _, cl, cells = tile.shape
    chan = groups * cl
    bw = 128
    rows = cells // bw + 2
    s = pl.program_id(0)
    edge = rim[:, rim.shape[1] - 1].reshape(chan, bw).astype(F32)
    edge = pltpu.roll(edge, lax.rem(bw - s * 12, bw), 1)
    lane = lax.broadcasted_iota(jnp.int32, (chan, bw), 1)
    for i in range(rows):
        if i == 0:
            mid = rim[:, 2 * s].reshape(chan, bw)
        elif i == rows - 1:
            mid = rim[:, 2 * s + 1].reshape(chan, bw)
        else:
            mid = tile[:, 0, :, (i - 1) * bw : i * bw].reshape(chan, bw)
        wide = mid.astype(F32)
        left = jnp.where(lane == 0, edge[:, i : i + 1], pltpu.roll(wide, 1, 1))
        right = jnp.where(lane == bw - 1, edge[:, rows + i : rows + i + 1], pltpu.roll(wide, bw - 1, 1))
        at = slice(i * bw, (i + 1) * bw)
        xs[0:chan, at] = left.astype(BF16)
        xs[chan : 2 * chan, at] = mid
        xs[2 * chan : 3 * chan, at] = right.astype(BF16)
    base = 9 * cl
    ident = eye(256, 256)
    cols = [nt(ident, pack[g, base + 2 * hl :, :]) for g in range(groups)]
    bias = jnp.concatenate([c[:cl, 1:2] for c in cols], axis=0)
    gain = jnp.concatenate([c[:cl, 2:3] for c in cols], axis=0)
    acc = jnp.zeros((chan, cells), F32)
    for a in range(3):
        for b in range(3):
            t = 3 * a + b
            w = pack[:, t * cl : (t + 1) * cl, :].reshape(chan, chan)
            acc += jnp.dot(
                w, xs[b * chan : (b + 1) * chan, a * bw : a * bw + cells], preferred_element_type=F32
            )
    acc = acc + bias
    squares = jnp.sum(acc * acc, axis=0, keepdims=True)
    normed = (acc * lax.rsqrt(squares / chan + norm_eps) * gain).astype(BF16)
    for g in range(groups):
        pre = jnp.dot(pack[g, base : base + hl, :], normed, preferred_element_type=F32)
        pre = pre + cols[g][:hl, 0:1]
        act = 0.5 * pre * (1.0 + lax.erf(pre * 0.7071067811865476))
        hid[g * hl : (g + 1) * hl, :] = act.astype(BF16)
    ow = pack[:, base + hl : base + 2 * hl, :].reshape(groups * hl, chan)
    upd = lax.dot_general(ow, hid[...], (((0,), (0,)), ((), ())), preferred_element_type=F32)
    out[:, 0] = upd.astype(BF16).reshape(groups, cl, cells)


def pick(index, table, which, out, wide, got, *, cl):
    s = pl.program_id(0)
    cells = got.shape[0]
    parts = 128 // cl

    @pl.when(s == 0)
    def _():
        wide[...] = table[...].astype(F32)

    def body(j, c):
        for u in range(16):
            at = j * 16 + u
            got[pl.ds(at, 1), :] = wide[pl.ds(index[s * cells + at], 1), :]
        return c

    lax.fori_loop(0, cells // 16, body, 0)
    rows = got[...].astype(BF16)
    part = which[0]
    total = jnp.zeros((cl, cells), F32)
    for k in range(parts):
        total = jnp.where(part == k, nt(eye(cl, 128, k * cl), rows), total)
    out[0] = total.astype(BF16)


def finish(rows, update, force, mask, scale, out, scr):
    cl, some, bh, bw = out.shape
    gain = scale[:, 0:1].astype(F32)
    for j in range(some):
        total = rows[j].astype(F32) + gain * update[j].astype(F32)
        total = (total + force[j].astype(F32)) * mask[j].astype(F32)
        for i in range(bh):
            scr[:, i, :] = total[:, i * bw : (i + 1) * bw]
        out[:, j] = scr[...].astype(BF16)


def on_device(
    ocean_state, atmos, flux_weight, conv_weight, conv_bias, norm_gain, in_weight, in_bias,
    out_weight, layer_scale, cell_mask, neighbours, remap,
):
    cl, slots, bh, bw = ocean_state.shape
    groups = lax.axis_size(("chan", "sec"))
    tiles = lax.axis_size("tile")
    chan = groups * cl
    hl = in_weight.shape[1]
    cells = bh * bw
    per = slots // groups
    some = 4

    state_spec = pl.BlockSpec((cl, some, bh, bw), lambda s, *_: (0, s, 0, 0))
    some_spec = pl.BlockSpec((some, cl, cells), lambda s, *_: (s, 0, 0))
    slot_spec = pl.BlockSpec((1, cl, cells), lambda s, *_: (s, 0, 0))
    rows, strips = pl.pallas_call(
        split_rows,
        grid=(slots // some,),
        in_specs=[state_spec],
        out_specs=[some_spec, whole(slots + 1, cl, 2 * bw)],
        out_shape=[
            jax.ShapeDtypeStruct((slots, cl, cells), BF16),
            jax.ShapeDtypeStruct((slots + 1, cl, 2 * bw), BF16),
        ],
        scratch_shapes=[pltpu.VMEM((cl, bh, bw), F32)],
        compiler_params=params(),
        name="split_rows",
    )(ocean_state)
    vec = jnp.stack(
        [jnp.pad(v, (0, chan - v.shape[0])) for v in (in_bias, conv_bias, norm_gain)]
    )
    vec = jnp.pad(vec, ((0, 13), (0, 0)))
    pack_rows = 9 * cl + 2 * hl + 16
    pack_local = pl.pallas_call(
        pack_weights,
        out_shape=jax.ShapeDtypeStruct((pack_rows, chan), BF16),
        compiler_params=params(),
        name="pack_weights",
    )(jnp.swapaxes(conv_weight, 1, 2), vec, in_weight, out_weight)
    pack = lax.all_gather(pack_local, ("chan", "sec"), axis=0)

    rows, strips, _ = lax.optimization_barrier((rows, strips, pack_local))
    resident = pl.BlockSpec(memory_space=pltpu.VMEM)
    tile, below, above = pl.pallas_call(
        exchange,
        in_specs=[resident, resident],
        out_specs=[resident] * 3,
        out_shape=[
            jax.ShapeDtypeStruct((groups, per, cl, cells), BF16),
            jax.ShapeDtypeStruct(strips.shape, BF16),
            jax.ShapeDtypeStruct(strips.shape, BF16),
        ],
        scratch_shapes=[
            pltpu.SemaphoreType.DMA((groups + 2,)),
            pltpu.SemaphoreType.DMA((groups + 2,)),
            pltpu.SemaphoreType.DMA,
        ],
        compiler_params=pltpu.CompilerParams(
            collective_id=0, has_side_effects=True, vmem_limit_bytes=LIMIT
        ),
        name="exchange",
    )(rows.reshape(groups, per, cl, cells), strips)
    below, above, atmos = lax.optimization_barrier((below, above, atmos))
    parts = 128 // cl
    trows = atmos.shape[0] // parts
    table = pl.pallas_call(
        flux_rows,
        out_shape=jax.ShapeDtypeStruct((trows, 128), BF16),
        compiler_params=params(),
        name="flux_rows",
    )(atmos, flux_weight.T)
    table = lax.all_gather(table, "tile", axis=0, tiled=True)

    local = lax.rem(remap, trows * parts)
    flat = (remap // (trows * parts)) * trows + lax.rem(local, trows)
    which = (local // trows).reshape(slots, 1, cells)
    lane_spec = pl.BlockSpec((1, 1, cells), lambda s, *_: (s, 0, 0))
    forcing = pl.pallas_call(
        functools.partial(pick, cl=cl),
        grid_spec=pltpu.PrefetchScalarGridSpec(
            num_scalar_prefetch=1,
            grid=(slots,),
            in_specs=[whole(tiles * trows, 128), lane_spec],
            out_specs=slot_spec,
            scratch_shapes=[pltpu.VMEM((tiles * trows, 128), F32), pltpu.VMEM((cells, 128), F32)],
        ),
        out_shape=jax.ShapeDtypeStruct((slots, cl, cells), BF16),
        compiler_params=params(),
        cost_estimate=pl.CostEstimate(flops=10**10, bytes_accessed=4 * 10**6, transcendentals=0),
        name="pick",
    )(flat.reshape(-1), table, which)

    first = (lax.axis_index("tile") - 1) * slots
    near = jnp.where(neighbours >= 0, jnp.clip(neighbours - first, 0, 3 * slots - 1), -1)
    strip_spec = whole(slots + 1, cl, 2 * bw)
    units = 2 * per + 1
    rim = pl.pallas_call(
        functools.partial(halo, per=per),
        grid_spec=pltpu.PrefetchScalarGridSpec(
            num_scalar_prefetch=1,
            grid=(groups,),
            in_specs=[strip_spec, strip_spec, strip_spec],
            out_specs=pl.BlockSpec((1, units, cl, bw), lambda s, *_: (s, 0, 0, 0)),
        ),
        out_shape=jax.ShapeDtypeStruct((groups, units, cl, bw), BF16),
        compiler_params=params(),
        name="halo",
    )(near, below, strips, above)
    rim = lax.all_to_all(rim, ("chan", "sec"), split_axis=0, concat_axis=0)
    update = pl.pallas_call(
        functools.partial(block, hl=hl),
        grid=(per,),
        in_specs=[
            pl.BlockSpec((groups, 1, cl, cells), lambda s: (0, s, 0, 0)),
            whole(groups, units, cl, bw),
            whole(groups, pack_rows, chan),
        ],
        out_specs=pl.BlockSpec((groups, 1, cl, cells), lambda s: (0, s, 0, 0)),
        out_shape=jax.ShapeDtypeStruct((groups, per, cl, cells), BF16),
        scratch_shapes=[
            pltpu.VMEM((3 * chan, (bh + 2) * bw), BF16),
            pltpu.VMEM((groups * hl, cells), BF16),
        ],
        compiler_params=params(),
        name="block",
    )(tile, rim, pack)
    update = lax.all_to_all(update, ("chan", "sec"), split_axis=0, concat_axis=0)
    return pl.pallas_call(
        finish,
        grid=(slots // some,),
        in_specs=[
            some_spec, some_spec, some_spec,
            pl.BlockSpec((some, 1, cells), lambda s: (s, 0, 0)), whole(cl, 1),
        ],
        out_specs=state_spec,
        out_shape=jax.ShapeDtypeStruct(ocean_state.shape, BF16),
        scratch_shapes=[pltpu.VMEM((cl, bh, bw), F32)],
        compiler_params=params(),
        name="finish",
    )(
        rows,
        update.reshape(slots, cl, cells),
        forcing,
        cell_mask.reshape(slots, 1, cells),
        layer_scale.reshape(cl, 1),
    )


def solution(mesh):
    placed = (
        P(("chan", "sec"), ("ens", "tile"), None, None),
        P(("ens", "tile"), None),
        P(None, ("chan", "sec")),
        P(None, None, ("chan", "sec")),
        P(("chan", "sec")),
        P(("chan", "sec")),
        P(None, ("chan", "sec")),
        P(("chan", "sec")),
        P(("chan", "sec"), None),
        P(("chan", "sec")),
        P("tile", None, None),
        P("tile", None),
        P("tile", None, None),
    )
    return jax.shard_map(
        on_device,
        mesh=mesh,
        in_specs=placed,
        out_specs=P(("chan", "sec"), ("ens", "tile"), None, None),
        check_vma=False,
    )
```
